256 devices in a mesh: dp: 8 (over z), sp: 32 (over y, x, core).
Axes of the slice: x: 4, y: 4, z: 8, core: 2. Of those that a mesh axis runs over, the one named last changes fastest.
Arguments:
- tokens: bfloat16 [65536, 2048], P(('dp', 'sp')), may hold values from -9 to 9
- qkv_weight: bfloat16 [2048, 3072], P(('dp', 'sp')), may hold values from -0.125 to 0.125
- route: int32 [65536], P(('dp', 'sp')), may hold values from 0 to 7, as said below
- offset: int32 [65536], P(('dp', 'sp')), may hold values from 0 to 8191, as said below
- doc_lengths: int32 [8, 16], P('dp'), may hold values from 1 to 2048, 8192 in all within a row
Outputs:
- attended: bfloat16 [65536, 2048], P(('dp', 'sp'))
The draws below stay inside these ranges and needn't reach their ends.
Inputs may be any that keep to these rules, and one draw needn't show every extreme that they name: `route`: at every sp index the loader tokens of all dp indices map one to one onto the group rows of that sp index; every device sends 64 rows to one group, none to another and 32 to each other group. offset // 256 is the sp index of the token's device; no two tokens share route and offset.
All inputs are finite; a program needn't handle non-finite values.
Results may differ from the reference program's by a relative error of at most 0.012.
The reference program's roundings to bfloat16 on the way count: a program that leaves them out, or rounds other values in their place, can miss the bound.
Values may be sent and summed in bfloat16 or wider, within the bound.
A program may use at most 64 MiB of HBM per device.

```python
import math
import jax
import jax.numpy as jnp
import numpy as np
from jax import lax

D = 2048
QUERY_HEADS = 16
KEY_VALUE_HEADS = 4
HEAD_SIZE = 128
NDOC = 16
TOK_DEV = 256
GROUP_TOKENS_SIZE = 8192
TOKENS = 65536
MOST = 2048
C3 = 3072
N_DP = 8
N_SP = 32


def regroup_plan(key):
    base = TOK_DEV // N_DP
    first_key, second_key, dest_key, source_key = jax.random.split(key, 4)
    first = jax.random.randint(first_key, (N_SP,), 0, N_DP)
    second = (first + jax.random.randint(second_key, (N_SP,), 1, N_DP)) % N_DP
    src = jnp.arange(N_DP, dtype=jnp.int32)
    counts = base + base * (src[None, None, :] == (src[None, :, None] + first[:, None, None]) % N_DP).astype(jnp.int32)
    counts = counts - base * (src[None, None, :] == (src[None, :, None] + second[:, None, None]) % N_DP).astype(jnp.int32)
    ends_src = jnp.cumsum(counts, axis=2)
    starts_src = ends_src - counts
    inbound = jnp.cumsum(counts, axis=1) - counts
    steps = jnp.arange(TOK_DEV, dtype=jnp.int32)
    sorted_route = jnp.sum((steps[None, None, :, None] >= ends_src[:, :, None, :]).astype(jnp.int32), axis=-1)
    chosen = sorted_route[..., None] == src[None, None, None, :]
    rank = steps[None, None, :] - jnp.sum(jnp.where(chosen, starts_src[:, :, None, :], 0), axis=-1)
    dest_row = jnp.sum(jnp.where(chosen, inbound[:, :, None, :], 0), axis=-1) + rank
    dest_perm = jax.vmap(lambda k: jax.random.permutation(k, TOK_DEV))(jax.random.split(dest_key, N_SP * N_DP))
    dest_perm = dest_perm.reshape(N_SP, N_DP, TOK_DEV).astype(jnp.int32)
    lanes = jnp.arange(N_SP, dtype=jnp.int32)[:, None, None]
    sorted_slot = dest_perm[lanes, sorted_route, dest_row]
    source_perm = jax.vmap(lambda k: jax.random.permutation(k, TOK_DEV))(jax.random.split(source_key, N_SP * N_DP))
    source_perm = source_perm.reshape(N_SP, N_DP, TOK_DEV).astype(jnp.int32)
    route_all = jnp.take_along_axis(sorted_route, source_perm, axis=2)
    slot_all = jnp.take_along_axis(sorted_slot, source_perm, axis=2)
    offset_all = lanes * TOK_DEV + slot_all
    route_all = jnp.transpose(route_all, (1, 0, 2)).reshape(TOKENS).astype(jnp.int32)
    offset_all = jnp.transpose(offset_all, (1, 0, 2)).reshape(TOKENS).astype(jnp.int32)
    return (route_all, offset_all)


def draw_route(key, part):
    return regroup_plan(key)[0]


def draw_offset(key, part):
    return regroup_plan(key)[1]


def draw_tokens(key, part):
    key = jax.random.fold_in(key, 7)
    value_key = jax.random.fold_in(key, 0)
    value_rows_local = jnp.clip(jax.random.normal(value_key, (TOKENS, D), jnp.float32), -6.0, 6.0)
    return value_rows_local.astype(jnp.bfloat16)


def shard_levels(key, extent, shards, least, top_value):
    level, own = 1.0, jax.random.fold_in(key, 6)
    for position, blocks in shards:
        heights = jnp.exp(jax.random.uniform(jax.random.fold_in(own, position), (blocks,), jnp.float32, least / len(shards), top_value / len(shards)))
        level = level * jnp.repeat(heights, extent[position] // blocks).reshape([-1 if axis == position else 1 for axis in range(len(extent))])
    return level


def length_profile(number_of, total, reach, skew):
    weights = [(1 << 20) // math.isqrt(grade ** skew) + 1 for grade in range(2, number_of + 1)]
    rest, given = total - reach - (number_of - 1), [1] * (number_of - 1)
    while rest > 0:
        free = [i for i in range(number_of - 1) if given[i] < reach]
        pool, remaining = sum([weights[i] for i in free]), rest
        for i in free:
            extra = min(reach - given[i], max(1, remaining * weights[i] // pool), rest)
            given[i] = given[i] + extra
            rest = rest - extra
    return np.array([reach] + given)


def uneven_parts(own_key, count, total, most, lean):
    if count == 2:
        one = jax.random.randint(own_key, (), max(1, total - most), min(most, total - 1) + 1)
        return jnp.stack([one, total - one])
    sizes = jnp.asarray(length_profile(count, total, most, lean), jnp.int32)
    pairs = (count - 1) // 2
    source_of, sink = sizes[1:1 + 2 * pairs:2], sizes[2:2 + 2 * pairs:2]
    margin = jnp.minimum(source_of - 1, most - sink)
    shifted = jax.random.randint(jax.random.fold_in(own_key, 1), (pairs,), 0, 1 << 20) % (margin + 1)
    sizes = sizes.at[1:1 + 2 * pairs:2].set(source_of - shifted).at[2:2 + 2 * pairs:2].set(sink + shifted)
    return sizes[jax.random.permutation(jax.random.fold_in(own_key, 2), count)]


def noise(own_key, extent, scale, most, cuts=(), held_as=jnp.bfloat16):
    gain = shard_levels(own_key, extent, cuts, -0.22, 0.18) if cuts else 1.0
    entries = jax.random.normal(own_key, extent, jnp.float32) * scale * gain
    return jnp.minimum(jnp.maximum(entries, -most), most).astype(held_as)


def setup_inputs(seed: int = 0) -> dict:
    streams_of = jax.random.split(jax.random.key(seed), 6)
    return {
        "tokens": draw_tokens(jax.random.fold_in(streams_of[5], 71), 0),
        "qkv_weight": noise(streams_of[1], (D, C3), D ** -0.5, 0.125, ((0, 256),)),
        "route": draw_route(jax.random.fold_in(streams_of[5], 71), 0),
        "offset": draw_offset(jax.random.fold_in(streams_of[5], 71), 0),
        "doc_lengths": jax.vmap(lambda own: uneven_parts(own, NDOC, GROUP_TOKENS_SIZE, MOST, 2))(jax.random.split(streams_of[4], N_DP)).reshape((N_DP, NDOC)).astype(jnp.int32),
    }


ROPE_BASE = 500000.0


def doc_positions(points, lens):
    ends = jnp.cumsum(lens)
    doc = jnp.sum((points[:, None] >= ends[None, :]).astype(jnp.int32), axis=1)
    starts = ends - lens
    picks = jnp.arange(lens.shape[0], dtype=jnp.int32)
    first = jnp.sum(jnp.where(doc[:, None] == picks[None, :], starts[None, :], 0), axis=1)
    return doc, points - first


def rotate(value_rows_local, pos):
    half = value_rows_local.shape[-1] // 2
    freq = ROPE_BASE ** (-(jnp.arange(half, dtype=jnp.float32) * 2.0 / value_rows_local.shape[-1]))
    angle = pos.astype(jnp.float32)[:, None] * freq[None, :]
    cosine = jnp.cos(angle)[:, None, :]
    sine = jnp.sin(angle)[:, None, :]
    first, second = value_rows_local[..., :half], value_rows_local[..., half:]
    return jnp.concatenate([first * cosine - second * sine, second * cosine + first * sine], axis=-1)


def reference(tokens, qkv_weight, route, offset, doc_lengths):
    dest = route * GROUP_TOKENS_SIZE + offset
    grouped = jnp.zeros_like(tokens).at[dest].set(tokens)
    grouped = grouped.reshape(N_DP, GROUP_TOKENS_SIZE, D)
    heads_per_group = QUERY_HEADS // KEY_VALUE_HEADS
    scale = HEAD_SIZE ** -0.5
    qblock = min(GROUP_TOKENS_SIZE, 512)
    window = min(GROUP_TOKENS_SIZE, MOST + qblock)
    nblocks = GROUP_TOKENS_SIZE // qblock

    def group_fn(args):
        rows, lens = args
        query_key_value = jnp.dot(rows, qkv_weight, preferred_element_type=jnp.float32).astype(jnp.bfloat16)
        points = jnp.arange(GROUP_TOKENS_SIZE, dtype=jnp.int32)
        doc, pos = doc_positions(points, lens)
        query = query_key_value[:, :QUERY_HEADS * HEAD_SIZE].reshape(GROUP_TOKENS_SIZE, QUERY_HEADS, HEAD_SIZE)
        key_rows_local = query_key_value[:, QUERY_HEADS * HEAD_SIZE:(QUERY_HEADS + KEY_VALUE_HEADS) * HEAD_SIZE].reshape(GROUP_TOKENS_SIZE, KEY_VALUE_HEADS, HEAD_SIZE)
        value_rows_local = query_key_value[:, (QUERY_HEADS + KEY_VALUE_HEADS) * HEAD_SIZE:].reshape(GROUP_TOKENS_SIZE, KEY_VALUE_HEADS, HEAD_SIZE)
        query = rotate(query.astype(jnp.float32), pos).astype(jnp.bfloat16)
        key_rows_local = rotate(key_rows_local.astype(jnp.float32), pos).astype(jnp.bfloat16)

        def head_fn(head):
            qh = lax.dynamic_index_in_dim(query, head, 1, keepdims=False)
            kh = lax.dynamic_index_in_dim(key_rows_local, head // heads_per_group, 1, keepdims=False)
            vh = lax.dynamic_index_in_dim(value_rows_local, head // heads_per_group, 1, keepdims=False)

            def block_fn(block):
                start = (block * qblock).astype(jnp.int32)
                lower = jnp.clip(start - MOST, 0, GROUP_TOKENS_SIZE - window).astype(jnp.int32)
                qrows = lax.dynamic_slice_in_dim(qh, start, qblock, 0)
                krows = lax.dynamic_slice_in_dim(kh, lower, window, 0)
                vrows = lax.dynamic_slice_in_dim(vh, lower, window, 0)
                qpoint = start + jnp.arange(qblock, dtype=jnp.int32)
                kpoint = lower + jnp.arange(window, dtype=jnp.int32)
                qdoc = lax.dynamic_slice_in_dim(doc, start, qblock, 0)
                kdoc = lax.dynamic_slice_in_dim(doc, lower, window, 0)
                allowed = (qdoc[:, None] == kdoc[None, :]) & (kpoint[None, :] <= qpoint[:, None])
                scores = jnp.einsum("qd,kd->qk", qrows.astype(jnp.float32), krows.astype(jnp.float32)) * scale
                scores = jnp.where(allowed, scores, -jnp.inf)
                top = jnp.max(scores, axis=1)
                weights = jnp.where(allowed, jnp.exp(scores - top[:, None]), 0.0)
                total = jnp.sum(weights, axis=1)
                summed = jnp.dot(weights.astype(jnp.bfloat16), vrows, preferred_element_type=jnp.float32)
                return (summed / total[:, None]).astype(jnp.bfloat16)

            out = lax.map(block_fn, jnp.arange(nblocks, dtype=jnp.int32))
            return out.reshape(GROUP_TOKENS_SIZE, HEAD_SIZE)

        heads = lax.map(head_fn, jnp.arange(QUERY_HEADS, dtype=jnp.int32))
        return jnp.transpose(heads, (1, 0, 2)).reshape(GROUP_TOKENS_SIZE, QUERY_HEADS * HEAD_SIZE)

    result = lax.map(group_fn, (grouped, doc_lengths))
    return result.reshape(TOKENS, QUERY_HEADS * HEAD_SIZE)
```

```python
import jax
import jax.numpy as jnp
from jax import lax
from jax.experimental import pallas as pl
from jax.experimental.pallas import tpu as pltpu
from jax.sharding import PartitionSpec as P

HEAD_SIZE = 128
ROPE_BASE = 500000.0
N_DP = 8
SIDE = 4
CHIPS = SIDE * SIDE
TOK = 256
CHIP_TOK = 2 * TOK
MODEL = 2048
SLOT = TOK // N_DP
QCOLS = 1024
KVCOLS = 256
COLS = QCOLS + 2 * KVCOLS
HALF = COLS // 2
REACH = 4
MESH = pl.DeviceIdType.MESH
F32 = jnp.float32
BF16 = jnp.bfloat16
I32 = jnp.int32


def iota(shape, dim):
    return lax.broadcasted_iota(I32, shape, dim)


class Copies:
    def __init__(self, send, recv):
        self.send, self.recv, self.made = send, recv, []

    def start(self, src, dst, device):
        n = len(self.made)
        copy = pltpu.make_async_remote_copy(
            src_ref=src,
            dst_ref=dst,
            send_sem=self.send.at[n],
            recv_sem=self.recv.at[n],
            device_id=device,
            device_id_type=MESH,
        )
        copy.start()
        self.made.append(copy)
        return copy

    def drain(self):
        for copy in self.made:
            copy.wait_send()


def meet(devices):
    barrier = pltpu.get_barrier_semaphore()
    for device in devices:
        pl.semaphore_signal(barrier, inc=1, device_id=device, device_id_type=MESH)
    pl.semaphore_wait(barrier, len(devices))


N_PROJECT = 1 + 7 + 2 * 7 + 2 * 7 + 2 * (4 + 16) + 1


def project_kernel(
    tokens, w, route, offset, cosine, sine, q_out, kv_out,
    packed, ids, got, got_ids, extra, extra_ids, wsend, wrecv, wbuf, x, send, recv,
):
    z = lax.axis_index("dp")
    sp = lax.axis_index("sp")
    core = lax.rem(sp, 2)
    chip = sp // 2
    cy, cx = chip // SIDE, lax.rem(chip, SIDE)
    partner = (z, sp + 1 - 2 * core)

    def at_z(d):
        return (lax.rem(z + d + N_DP, N_DP), sp)

    def place(dy, dx):
        return lax.rem(cy + dy + SIDE, SIDE) * SIDE + lax.rem(cx + dx + SIDE, SIDE)

    def at_chip(dy, dx):
        return (z, place(dy, dx) * 2 + core)

    def half_of(c):
        cols = lambda base, width: w[:, pl.ds(pl.multiple_of(base + c * width, 128), width)]
        return [
            (0, QCOLS, cols(0, QCOLS)),
            (QCOLS, KVCOLS, cols(2 * QCOLS, KVCOLS)),
            (QCOLS + KVCOLS, KVCOLS, cols(2 * QCOLS + 2 * KVCOLS, KVCOLS)),
        ]

    for base, width, part in half_of(1 - core):
        wsend[:, base : base + width] = part.astype(F32)

    meet(
        [at_z(d) for d in range(1, N_DP)]
        + [partner]
        + [at_chip(0, 1), at_chip(0, -1), at_chip(1, 0), at_chip(-1, 0)]
    )
    copies = Copies(send, recv)

    swap = copies.start(wsend, wrecv, partner)

    group = iota((8, TOK), 0)
    route_row = route[...]
    onehot = route_row == group
    before = (iota((TOK, TOK), 0) < iota((TOK, TOK), 1)).astype(F32).astype(BF16)
    rank = jnp.dot(
        onehot.astype(F32).astype(BF16), before, preferred_element_type=F32
    ).astype(I32)
    dest = jnp.where(rank < SLOT, group * SLOT + rank, N_DP * SLOT + rank - SLOT)
    dest = jnp.sum(jnp.where(onehot, dest, 0), axis=0, keepdims=True)

    swap.wait_recv()
    for base, width, part in half_of(core):
        own = part.astype(F32)
        other = wrecv[:, base : base + width]
        top = jnp.where(core == 0, own, other)
        bottom = jnp.where(core == 0, other, own)
        wbuf[z, chip, :, base : base + width] = jnp.concatenate([top, bottom], axis=0).astype(BF16)
    wz = [copies.start(wbuf.at[z, chip], wbuf.at[z, chip], at_z(d)) for d in range(1, N_DP)]

    for block in range(N_DP + 1):
        pick = (iota((SLOT, TOK), 0) + block * SLOT == dest).astype(F32).astype(BF16)
        packed[block] = jnp.dot(pick, tokens[...], preferred_element_type=F32).astype(BF16)
    extra[z] = packed[N_DP]

    def ring(s):
        out = []
        right, left = lax.rem(z - s + N_DP, N_DP), lax.rem(z + s, N_DP)
        out.append(copies.start(extra.at[right], extra.at[right], at_z(1)))
        if s < 3:
            out.append(copies.start(extra.at[left], extra.at[left], at_z(-1)))
        return out

    tours = [ring(0)]
    tokens_sent = []
    for d in range(1, N_DP):
        to = lax.rem(z + d, N_DP)
        tokens_sent.append(copies.start(packed.at[to], got.at[z], at_z(d)))
    got[z] = packed[z]

    facts = jnp.where(
        group == 0,
        offset[...] - sp * TOK,
        jnp.where(group == 1, route_row, jnp.where(group == 2, 1, 0)),
    ).astype(F32).astype(BF16)
    lane = iota((TOK, TOK), 0) - z * SLOT
    lane_ok = jnp.where((lane >= 0) & (lane < SLOT), lane, -10 * TOK)
    for block in range(N_DP + 1):
        pick = (lane_ok + block * SLOT == dest).astype(F32).astype(BF16)
        found = lax.dot_general(
            facts, pick, (((1,), (1,)), ((), ())), preferred_element_type=F32
        ).astype(I32)
        number = found[1:2] * TOK + found[0:1] + found[2:3]
        ids[block] = jnp.broadcast_to(number, (8, TOK))
    got_ids[z] = ids[z]
    ids_sent = []
    for d in range(1, N_DP):
        to = lax.rem(z + d, N_DP)
        ids_sent.append(copies.start(ids.at[to], got_ids.at[z], at_z(d)))
    extra_ids[z] = ids[N_DP]
    for d in range(1, N_DP):
        ids_sent.append(copies.start(extra_ids.at[z], extra_ids.at[z], at_z(d)))

    for copy in wz:
        copy.wait_recv()

    class Plane:
        def __init__(self, which, first, second):
            self.which, self.first, self.second = which, first, second

        def at(self, a, b):
            return (a * self.first[0] + b * self.second[0], a * self.first[1] + b * self.second[1])

        def send(self, a, b, z0, zn, to):
            ref = wbuf.at[
                pl.ds(z0, zn), place(*self.at(a, b)), :, pl.ds(self.which * HALF, HALF)
            ]
            return copies.start(ref, ref, at_chip(*self.at(*to)))

        def open(self):
            self.near = [self.send(0, 0, 0, 8, (1, 0)), self.send(0, 0, 0, 8, (-1, 0))]
            self.across = {}

        def spread(self, u):
            self.across[u] = [self.send(u, 0, 0, 8, (0, 1)), self.send(u, 0, 0, 8, (0, -1))]

        def forward(self):
            self.near[0].wait_recv()
            self.far = [self.send(-1, 0, 0, 4, (1, 0))]
            self.near[1].wait_recv()
            self.far.append(self.send(1, 0, 4, 4, (-1, 0)))

        def close(self):
            for copy in self.far:
                copy.wait_recv()

        def pass_on(self, u):
            self.across[u][0].wait_recv()
            one = self.send(u, -1, 0, 4, (0, 1))
            self.across[u][1].wait_recv()
            return [one, self.send(u, 1, 4, 4, (0, -1))]

    planes = [Plane(0, (0, 1), (1, 0)), Plane(1, (1, 0), (0, 1))]

    def ring_step(s):
        for copy in tours[-1]:
            copy.wait_recv()
        if s < 4:
            tours.append(ring(s))

    for plane in planes:
        plane.open()
    for plane in planes:
        plane.spread(0)
    for plane in planes:
        plane.forward()
    ring_step(1)
    for plane in planes:
        plane.spread(-1)
        plane.spread(1)
    for plane in planes:
        plane.close()
        plane.spread(2)
    last = []
    for u in (0, -1, 1, 2):
        for plane in planes:
            last.extend(plane.pass_on(u))
        if u == 0:
            ring_step(2)
        if u == -1:
            ring_step(3)
        if u == 1:
            ring_step(4)

    for copy in tokens_sent + ids_sent:
        copy.wait_recv()
    mine = iota((TOK, TOK), 0) + z * TOK + 1
    total = jnp.zeros((8, TOK), I32)
    more = jnp.zeros((8, TOK), I32)
    for source in range(N_DP):
        total += got_ids[source]
        more += extra_ids[source]
    to_place = (total[0:1] == mine).astype(F32).astype(BF16)
    to_place_more = (more[0:1] == mine).astype(F32).astype(BF16)
    own_rows = pl.ds(pl.multiple_of(core * TOK, TOK), TOK)
    for part in range(4):
        cols = slice(part * 512, part * 512 + 512)
        rows = jnp.dot(
            to_place, got[:, :, cols].reshape(TOK, 512), preferred_element_type=F32
        ) + jnp.dot(
            to_place_more, extra[:, :, cols].reshape(TOK, 512), preferred_element_type=F32
        )
        x[own_rows, cols] = rows.astype(BF16)
    shared = copies.start(x.at[own_rows], x.at[own_rows], partner)
    for copy in last:
        copy.wait_recv()
    shared.wait_recv()

    def project(c):
        cols = pl.ds(pl.multiple_of(c * 256, 256), 256)
        weights = wbuf[:, :, :, cols].reshape(MODEL, 256)
        return jnp.dot(x[...], weights, preferred_element_type=F32).astype(BF16)

    def rotated(y):
        parts = []
        for head in range(2):
            v = y[:, head * 128 : head * 128 + 128].astype(F32)
            parts.append((v * cosine[...] + pltpu.roll(v, 64, 1) * sine[...]).astype(BF16))
        return jnp.concatenate(parts, axis=1)

    kv_out[:, 0:256] = rotated(project(4))
    kv_out[:, 256:512] = project(5)

    def query(c, carry):
        q_out[:, pl.ds(pl.multiple_of(c * 256, 256), 256)] = rotated(project(c))
        return carry

    lax.fori_loop(0, 4, query, 0)
    copies.drain()


NEG = -1e30


def attend_kernel(q, kv, lens, out, kvbuf, keep, keep0, top, total, acc, mine, send, recv):
    z = lax.axis_index("dp")
    sp = lax.axis_index("sp")
    core = lax.rem(sp, 2)
    chip = sp // 2
    partner = (z, sp + 1 - 2 * core)

    def at_chip(d):
        return (z, lax.rem(chip + d + CHIPS, CHIPS) * 2 + core)

    meet(
        [at_chip(d) for d in range(1, REACH + 1)]
        + [at_chip(-d) for d in range(1, REACH + 1)]
        + [partner]
    )
    copies = Copies(send, recv)
    blocks = [copies.start(kv, kvbuf.at[d - 1], at_chip(d)) for d in range(1, REACH + 1)]

    row = iota((CHIP_TOK, 128), 0)
    first = jnp.zeros((CHIP_TOK, 128), I32)
    begin = lens[0, 0] * 0
    for e in range(16):
        first = jnp.where(row + chip * CHIP_TOK >= begin, begin, first)
        begin = begin + lens[0, e]
    first = first - chip * CHIP_TOK
    for t in range(4):
        col = iota((CHIP_TOK, 128), 1) + 128 * t
        keep[:, t * 128 : t * 128 + 128] = col - first
        keep0[:, t * 128 : t * 128 + 128] = jnp.where(col <= row, col - first, -1)

    factor = HEAD_SIZE ** (-0.5) * 1.4426950408889634

    def block_step(d, h):
        source = kv if d == 0 else kvbuf.at[d - 1]
        kcols = pl.ds(pl.multiple_of(h // 4 * 128, 128), 128)
        vcols = pl.ds(pl.multiple_of(256 + h // 4 * 128, 128), 128)
        qcols = pl.ds(pl.multiple_of(h * 128, 128), 128)
        for half in range(2):
            rows = slice(half * 256, half * 256 + 256)
            lo, hi = 0, 512
            if d == 0 and half == 0:
                hi = 256
            if d == REACH and half == 1:
                lo = 256
            keys = source[lo:hi, kcols]
            values = source[lo:hi, vcols]
            s = lax.dot_general(
                q[rows, qcols], keys, (((1,), (1,)), ((), ())), preferred_element_type=F32
            )
            seen = keep0[rows, lo:hi] >= 0 if d == 0 else keep[rows, lo:hi] >= 512 * d
            s = jnp.where(seen, s, NEG)
            best = s[:, 0:128]
            for t in range(1, (hi - lo) // 128):
                best = jnp.maximum(best, s[:, t * 128 : t * 128 + 128])
            best = jnp.broadcast_to(jnp.max(best, axis=1, keepdims=True), (256, 128))
            if d > 0:
                old = top[h, rows]
                best = jnp.maximum(old, best)
                alpha = jnp.exp2((old - best) * factor)
            part, weights = None, []
            for t in range((hi - lo) // 128):
                e = jnp.exp2((s[:, t * 128 : t * 128 + 128] - best) * factor)
                part = e if part is None else part + e
                weights.append(e.astype(BF16))
            pv = jnp.dot(jnp.concatenate(weights, axis=1), values, preferred_element_type=F32)
            if d > 0:
                part = total[h, rows] * alpha + part
                pv = acc[h, rows] * alpha + pv
            if d < REACH:
                top[h, rows] = best
                total[h, rows] = part
                acc[h, rows] = pv
            else:
                result = pv / jnp.sum(part, axis=1, keepdims=True)
                mine[rows, qcols] = result.astype(BF16)

    for d in range(REACH + 1):
        if d > 0:
            blocks[d - 1].wait_recv()

        def head(h, carry, d=d):
            block_step(d, h)
            return carry

        lax.fori_loop(0, 8, head, 0)

    own = pl.ds(pl.multiple_of(core * TOK, TOK), TOK)
    other = pl.ds(pl.multiple_of((1 - core) * TOK, TOK), TOK)
    cols = pl.ds(pl.multiple_of(core * QCOLS, QCOLS), QCOLS)
    back = copies.start(mine.at[other], out.at[:, cols], partner)
    out[:, cols] = mine[own]
    back.wait_recv()
    copies.drain()


def on_device(tokens, qkv_weight, route, offset, doc_lengths):
    chip = lax.axis_index("sp") // 2
    lens = doc_lengths
    ends = jnp.cumsum(lens[0])
    points = chip * CHIP_TOK + jnp.arange(CHIP_TOK, dtype=I32)
    starts = ends - lens[0]
    first = jnp.max(jnp.where(points[:, None] >= starts[None, :], starts[None, :], 0), axis=1)
    pos = points - first
    half = HEAD_SIZE // 2
    freq = ROPE_BASE ** (-(jnp.arange(half, dtype=F32) * 2.0 / HEAD_SIZE))
    angle = pos.astype(F32)[:, None] * freq[None, :]
    cosine, sine = jnp.cos(angle), jnp.sin(angle)
    cosine = jnp.concatenate([cosine, cosine], axis=1)
    sine = jnp.concatenate([-sine, sine], axis=1)

    vmem = pl.BlockSpec(memory_space=pltpu.VMEM)
    q, kv = pl.pallas_call(
        project_kernel,
        out_shape=(
            jax.ShapeDtypeStruct((CHIP_TOK, QCOLS), BF16),
            jax.ShapeDtypeStruct((CHIP_TOK, 2 * KVCOLS), BF16),
        ),
        in_specs=[vmem] * 6,
        out_specs=(vmem, vmem),
        scratch_shapes=[
            pltpu.VMEM((N_DP + 1, SLOT, MODEL), BF16),
            pltpu.VMEM((N_DP + 1, 8, TOK), I32),
            pltpu.VMEM((N_DP, SLOT, MODEL), BF16),
            pltpu.VMEM((N_DP, 8, TOK), I32),
            pltpu.VMEM((N_DP, SLOT, MODEL), BF16),
            pltpu.VMEM((N_DP, 8, TOK), I32),
            pltpu.VMEM((8, COLS), F32),
            pltpu.VMEM((8, COLS), F32),
            pltpu.VMEM((N_DP, CHIPS, 16, COLS), BF16),
            pltpu.VMEM((CHIP_TOK, MODEL), BF16),
            pltpu.SemaphoreType.DMA((N_PROJECT,)),
            pltpu.SemaphoreType.DMA((N_PROJECT,)),
        ],
        compiler_params=pltpu.CompilerParams(
            collective_id=0, has_side_effects=True, vmem_limit_bytes=48 * 2**20
        ),
    )(tokens, qkv_weight, route.reshape(1, TOK), offset.reshape(1, TOK), cosine, sine)

    return pl.pallas_call(
        attend_kernel,
        out_shape=jax.ShapeDtypeStruct((TOK, 2 * QCOLS), BF16),
        in_specs=[vmem, vmem, pl.BlockSpec(memory_space=pltpu.SMEM)],
        out_specs=vmem,
        scratch_shapes=[
            pltpu.VMEM((REACH, CHIP_TOK, 2 * KVCOLS), BF16),
            pltpu.VMEM((CHIP_TOK, CHIP_TOK), I32),
            pltpu.VMEM((CHIP_TOK, CHIP_TOK), I32),
            pltpu.VMEM((8, CHIP_TOK, 128), F32),
            pltpu.VMEM((8, CHIP_TOK, 128), F32),
            pltpu.VMEM((8, CHIP_TOK, 128), F32),
            pltpu.VMEM((CHIP_TOK, QCOLS), BF16),
            pltpu.SemaphoreType.DMA((REACH + 1,)),
            pltpu.SemaphoreType.DMA((REACH + 1,)),
        ],
        compiler_params=pltpu.CompilerParams(
            collective_id=1, has_side_effects=True, vmem_limit_bytes=48 * 2**20
        ),
    )(q, kv, lens)


def solution(mesh):
    in_specs = (
        P(("dp", "sp"), None),
        P(("dp", "sp"), None),
        P(("dp", "sp")),
        P(("dp", "sp")),
        P("dp", None),
    )
    out_specs = P(("dp", "sp"), None)
    return jax.shard_map(
        on_device, mesh=mesh, in_specs=in_specs, out_specs=out_specs, check_vma=False
    )
```

```python
import jax
import jax.numpy as jnp
from jax import lax
from jax.experimental import pallas as pl
from jax.experimental.pallas import tpu as pltpu
from jax.sharding import PartitionSpec as P

HEAD_SIZE = 128
ROPE_BASE = 500000.0
N_DP = 8
SIDE = 4
CHIPS = SIDE * SIDE
TOK = 256
CHIP_TOK = 2 * TOK
MODEL = 2048
SLOT = TOK // N_DP
QCOLS = 1024
KVCOLS = 256
COLS = QCOLS + 2 * KVCOLS
HALF = COLS // 2
REACH = 4
HEADS_AT_ONCE = 2
DOCS = 16
PIECES = 4
LEGS = 7
BIG = 2.0**100
FACTOR = HEAD_SIZE ** (-0.5) * 1.4426950408889634
EXTRA_RIGHT, EXTRA_LEFT = 3, 4
W_RIGHT, W_LEFT = 3, 4
MESH = pl.DeviceIdType.MESH
F32 = jnp.float32
BF16 = jnp.bfloat16
I32 = jnp.int32


def iota(shape, dim):
    return lax.broadcasted_iota(I32, shape, dim)


class Copies:
    def __init__(self, send, recv):
        self.send, self.recv, self.made = send, recv, []

    def start(self, src, dst, device):
        n = len(self.made)
        copy = pltpu.make_async_remote_copy(
            src_ref=src,
            dst_ref=dst,
            send_sem=self.send.at[n],
            recv_sem=self.recv.at[n],
            device_id=device,
            device_id_type=MESH,
        )
        copy.start()
        self.made.append(copy)
        return copy

    def drain(self):
        for copy in self.made:
            copy.wait_send()


def meet(devices):
    barrier = pltpu.get_barrier_semaphore()
    for device in devices:
        pl.semaphore_signal(barrier, inc=1, device_id=device, device_id_type=MESH)
    pl.semaphore_wait(barrier, len(devices))


N_COPIES = 1 + 7 + 7 + 7 + 7 + 2 * (4 + 16) + 1 + 2


def kernel(
    tokens, w, route, offset, lens, freq, out,
    packed, ids, got, got_ids, extra, wsend, wrecv, wbuf, x,
    cosine, sine, q, kv, kvbuf, qdoc, kdoc, top, total, acc, mine,
    send, recv, leg_send, leg_recv,
):
    z = lax.axis_index("dp")
    sp = lax.axis_index("sp")
    core = lax.rem(sp, 2)
    chip = sp // 2
    cy, cx = chip // SIDE, lax.rem(chip, SIDE)
    partner = (z, sp + 1 - 2 * core)

    def at_z(d):
        return (lax.rem(z + d + N_DP, N_DP), sp)

    def place(dy, dx):
        return lax.rem(cy + dy + SIDE, SIDE) * SIDE + lax.rem(cx + dx + SIDE, SIDE)

    def at_chip(dy, dx):
        return (z, place(dy, dx) * 2 + core)

    def half_of(c):
        cols = lambda base, width: w[:, pl.ds(pl.multiple_of(base + c * width, 128), width)]
        return [
            (0, QCOLS, cols(0, QCOLS)),
            (QCOLS, KVCOLS, cols(2 * QCOLS, KVCOLS)),
            (QCOLS + KVCOLS, KVCOLS, cols(2 * QCOLS + 2 * KVCOLS, KVCOLS)),
        ]

    for base, width, part in half_of(1 - core):
        wsend[:, base : base + width] = part.astype(F32)

    meet(
        [at_z(d) for d in range(1, N_DP)]
        + [partner]
        + [at_chip(0, 1), at_chip(0, -1), at_chip(1, 0), at_chip(-1, 0)]
    )
    copies = Copies(send, recv)

    swap = copies.start(wsend, wrecv, partner)

    group = iota((8, TOK), 0)
    route_row = route[...]
    onehot = route_row == group
    before = (iota((TOK, TOK), 0) < iota((TOK, TOK), 1)).astype(F32).astype(BF16)
    rank = jnp.dot(
        onehot.astype(F32).astype(BF16), before, preferred_element_type=F32
    ).astype(I32)
    dest = jnp.where(rank < SLOT, group * SLOT + rank, N_DP * SLOT + rank - SLOT)
    dest = jnp.sum(jnp.where(onehot, dest, 0), axis=0, keepdims=True)

    def pack(block):
        pick = (iota((SLOT, TOK), 0) + block * SLOT == dest).astype(F32).astype(BF16)
        return jnp.dot(pick, tokens[...], preferred_element_type=F32).astype(BF16)

    def ring(ref, s, right_steps, left_steps):
        sent = []
        right, left = lax.rem(z - s + N_DP, N_DP), lax.rem(z + s, N_DP)
        if s < right_steps:
            sent.append(copies.start(ref(right), ref(right), at_z(1)))
        if s < left_steps:
            sent.append(copies.start(ref(left), ref(left), at_z(-1)))
        return sent

    def extra_ring(s):
        return ring(lambda i: extra.at[i], s, EXTRA_RIGHT, EXTRA_LEFT)

    def w_ring(s):
        return ring(lambda i: wbuf.at[i, chip], s, W_RIGHT, W_LEFT)

    swap.wait_recv()
    for base, width, part in half_of(core):
        own = part.astype(F32)
        other = wrecv[:, base : base + width]
        first = jnp.where(core == 0, own, other)
        second = jnp.where(core == 0, other, own)
        wbuf[z, chip, :, base : base + width] = jnp.concatenate([first, second], axis=0).astype(BF16)
    w_tour = w_ring(0)

    facts = jnp.where(
        group == 0,
        offset[...] - sp * TOK,
        jnp.where(group == 1, route_row, jnp.where(group == 2, 1, 0)),
    ).astype(F32).astype(BF16)
    lane = iota((TOK, TOK), 0) - z * SLOT
    lane_ok = jnp.where((lane >= 0) & (lane < SLOT), lane, -10 * TOK)

    def numbers_of(block):
        pick = (lane_ok + block * SLOT == dest).astype(F32).astype(BF16)
        found = lax.dot_general(
            facts, pick, (((1,), (1,)), ((), ())), preferred_element_type=F32
        ).astype(I32)
        number = found[1:2] * TOK + found[0:1] + found[2:3]
        return [number[:, 0:128], number[:, 128:256]]

    extra[z] = pack(N_DP)
    more = numbers_of(N_DP) + [jnp.zeros((4, 128), I32)]

    def prepare(d):
        to = lax.rem(z + d, N_DP)
        packed[to] = pack(to)
        ids[to] = jnp.concatenate(numbers_of(to) + more, axis=0)

    def w_step(s):
        for copy in w_tour:
            copy.wait_recv()
        return w_ring(s)

    prepare(4)
    w_tour = w_step(1)
    prepare(3)
    prepare(5)
    w_tour = w_step(2)
    prepare(2)
    prepare(6)
    w_tour = w_step(3)
    prepare(1)
    prepare(7)
    w_tour = w_step(4)

    tokens_sent = []

    def send_tokens(d):
        to = lax.rem(z + d, N_DP)
        tokens_sent.append(copies.start(packed.at[to], got.at[z], at_z(d)))
        tokens_sent.append(copies.start(ids.at[to], got_ids.at[z], at_z(d)))

    def extra_step(s):
        for copy in tour:
            copy.wait_recv()
        return extra_ring(s)

    tour = extra_ring(0)
    send_tokens(4)

    class Plane:
        def __init__(self, which, first, second):
            self.which, self.first, self.second = which, first, second

        def at(self, a, b):
            return (a * self.first[0] + b * self.second[0], a * self.first[1] + b * self.second[1])

        def send(self, a, b, z0, zn, to):
            ref = wbuf.at[
                pl.ds(z0, zn), place(*self.at(a, b)), :, pl.ds(self.which * HALF, HALF)
            ]
            return copies.start(ref, ref, at_chip(*self.at(*to)))

        def open(self):
            self.near = [self.send(0, 0, 0, 8, (1, 0)), self.send(0, 0, 0, 8, (-1, 0))]
            self.across = {}

        def spread(self, u):
            self.across[u] = [self.send(u, 0, 0, 8, (0, 1)), self.send(u, 0, 0, 8, (0, -1))]

        def forward(self):
            self.near[0].wait_recv()
            self.far = [self.send(-1, 0, 0, 4, (1, 0))]
            self.near[1].wait_recv()
            self.far.append(self.send(1, 0, 4, 4, (-1, 0)))

        def close(self):
            for copy in self.far:
                copy.wait_recv()

        def pass_on(self, u):
            self.across[u][0].wait_recv()
            one = self.send(u, -1, 0, 4, (0, 1))
            self.across[u][1].wait_recv()
            return [one, self.send(u, 1, 4, 4, (0, -1))]

    planes = [Plane(0, (0, 1), (1, 0)), Plane(1, (1, 0), (0, 1))]
    for plane in planes:
        plane.open()
    for plane in planes:
        plane.spread(0)

    prepare(0)
    got[z] = packed[z]
    got_ids[z] = ids[z]
    tour = extra_step(1)
    send_tokens(3)
    send_tokens(5)
    for plane in planes:
        plane.forward()
    for plane in planes:
        plane.spread(-1)
        plane.spread(1)

    tour = extra_step(2)
    send_tokens(2)
    send_tokens(6)

    lanes = iota((1, 128), 1)
    starts = jnp.full((1, 128), 2**30, I32)
    ends = jnp.full((1, 128), 2**30, I32)
    row = iota((CHIP_TOK, 128), 0) + chip * CHIP_TOK
    begin_of = jnp.zeros((CHIP_TOK, 128), I32)
    begin = lens[0, 0] * 0
    for e in range(DOCS):
        starts = jnp.where(lanes == e, begin, starts)
        begin_of = jnp.where(row >= begin, begin, begin_of)
        begin = begin + lens[0, e]
        ends = jnp.where(lanes == e, begin, ends)
    angle = (row - begin_of).astype(F32) * freq[...]
    cosine[...] = jnp.cos(angle)
    sine[...] = jnp.sin(angle) * jnp.where(lanes < 64, -1.0, 1.0)

    def member(base):
        point = iota((CHIP_TOK, 128), 0) + base
        return (point >= starts) & (point < ends)

    qdoc[...] = jnp.where(member(chip * CHIP_TOK), 1.0, 0.0).astype(BF16)
    for d in range(REACH + 1):
        kdoc[d] = jnp.where(member((chip - d) * CHIP_TOK), 0.0, -BIG).astype(BF16)

    for plane in planes:
        plane.close()
        plane.spread(2)
    last = []

    def pass_on(u):
        for plane in planes:
            last.extend(plane.pass_on(u))

    pass_on(0)
    tour = extra_step(3)
    send_tokens(1)
    send_tokens(7)
    pass_on(-1)
    pass_on(1)
    tour = extra_step(4)
    pass_on(2)

    for copy in tokens_sent:
        copy.wait_recv()
    mine_ids = iota((TOK, TOK), 0) + z * TOK + 1
    numbers = jnp.zeros((8, 128), I32)
    for source in range(N_DP):
        numbers += got_ids[source]
    to_place = [
        (jnp.concatenate([numbers[n : n + 1], numbers[n + 1 : n + 2]], axis=1) == mine_ids)
        .astype(F32)
        .astype(BF16)
        for n in (0, 2)
    ]
    own_rows = pl.ds(pl.multiple_of(core * TOK, TOK), TOK)
    other_rows = pl.ds(pl.multiple_of((1 - core) * TOK, TOK), TOK)
    for part in range(4):
        cols = slice(part * 512, part * 512 + 512)
        rows = jnp.dot(
            to_place[0], got[:, :, cols].reshape(TOK, 512), preferred_element_type=F32
        ) + jnp.dot(
            to_place[1], extra[:, :, cols].reshape(TOK, 512), preferred_element_type=F32
        )
        x[own_rows, cols] = rows.astype(BF16)
    shared = copies.start(x.at[own_rows], x.at[own_rows], partner)
    for copy in last:
        copy.wait_recv()

    def project(c, rows):
        cols = pl.ds(pl.multiple_of(c * 256, 256), 256)
        weights = wbuf[:, :, :, cols].reshape(MODEL, 256)
        return jnp.dot(x[rows], weights, preferred_element_type=F32).astype(BF16)

    def rotated(y, rows):
        parts = []
        for n in range(2):
            v = y[:, n * 128 : n * 128 + 128].astype(F32)
            parts.append((v * cosine[rows] + pltpu.roll(v, 64, 1) * sine[rows]).astype(BF16))
        return parts

    def project_keys(rows, base):
        keys = rotated(project(4, rows), rows)
        values = project(5, rows).astype(F32)
        for g in range(2):
            kv[2 * g, rows] = keys[g]
            for t in range(2):
                block = values[t * 128 : t * 128 + 128, g * 128 : g * 128 + 128]
                at = pl.ds(pl.multiple_of(base + t * 128, 128), 128)
                kv[2 * g + 1, at] = block.T.astype(BF16)

    project_keys(own_rows, core * TOK)
    shared.wait_recv()
    project_keys(other_rows, (1 - core) * TOK)

    def leg(n, number, d, to, source, when):
        copy = pltpu.make_async_remote_copy(
            src_ref=source,
            dst_ref=kvbuf.at[d - 1, n],
            send_sem=leg_send.at[n, number],
            recv_sem=leg_recv.at[n, d - 1],
            device_id=to,
            device_id_type=MESH,
        )
        return copy, when

    def legs(n):
        own, came = kv.at[n], lambda d: kvbuf.at[d - 1, n]
        inner = (cx == 1) | (cx == 2)
        return [
            leg(n, 0, 4, at_chip(1, 0), own, None),
            leg(n, 1, 1, at_chip(0, 1), own, cx < 3),
            leg(n, 2, 3, at_chip(0, -1), own, cx == 0),
            leg(n, 3, 3, at_chip(0, -1), came(4), cx > 0),
            leg(n, 4, 1, at_chip(0, 1), came(4), cx == 3),
            leg(n, 5, 2, at_chip(0, 1), came(1), inner),
            leg(n, 6, 2, at_chip(0, -1), came(3), inner),
        ]

    routes = [legs(n) for n in range(PIECES)]

    def do(action, n, number):
        copy, when = routes[n][number]
        run = copy.start if action == "start" else copy.wait_send
        if when is None:
            run()
        else:
            pl.when(when)(run)

    def arrived(n, d):
        pltpu.make_async_remote_copy(
            src_ref=kvbuf.at[d - 1, n],
            dst_ref=kvbuf.at[d - 1, n],
            send_sem=leg_send.at[n, 0],
            recv_sem=leg_recv.at[n, d - 1],
            device_id=partner,
            device_id_type=MESH,
        ).wait_recv()
        for number in {4: (3, 4), 1: (5,), 3: (6,), 2: ()}[d]:
            do("start", n, number)

    for n in range(PIECES):
        for number in range(3):
            do("start", n, number)

    def query(c, carry):
        for n, part in enumerate(rotated(project(c, slice(0, CHIP_TOK)), slice(0, CHIP_TOK))):
            q[:, pl.ds(pl.multiple_of(c * 256 + n * 128, 128), 128)] = part
        return carry

    lax.fori_loop(0, 4, query, 0)

    def block_step(d, g, heads, first, last):
        keys_of = kv.at[2 * g] if d == 0 else kvbuf.at[d - 1, 2 * g]
        values_of = kv.at[2 * g + 1] if d == 0 else kvbuf.at[d - 1, 2 * g + 1]
        chains = []
        for r in heads:
            h = g * 4 + r
            qcols = pl.ds(pl.multiple_of(h * 128, 128), 128)
            for half in range(2):
                lo, hi = 0, 512
                if d == 0 and half == 0:
                    hi = 256
                if d == REACH and half == 1:
                    lo = 256
                chains.append((h, qcols, slice(half * 256, half * 256 + 256), half, lo, hi))
        scores, old = [], []
        for h, qcols, qs, half, lo, hi in chains:
            keys = jnp.concatenate([keys_of[lo:hi], kdoc[d, lo:hi]], axis=1)
            query = jnp.concatenate([q[qs, qcols], qdoc[qs]], axis=1)
            s = lax.dot_general(
                keys, query, (((1,), (1,)), ((), ())), preferred_element_type=F32
            )
            if d == 0:
                n = hi - lo
                seen = iota((n, 256), 0) + lo <= iota((n, 256), 1) + half * 256
                s = jnp.where(seen, s, -BIG)
            scores.append(s)
            if not first:
                old.append((top[h, :, qs], total[h, :, qs], acc[h, :, qs]))
        new = []
        for n, (h, qcols, qs, half, lo, hi) in enumerate(chains):
            s = scores[n]
            best = jnp.max(s, axis=0, keepdims=True)
            if not first:
                best = jnp.maximum(old[n][0], best)
                alpha = jnp.exp2((old[n][0] - best) * FACTOR)
            e = jnp.exp2((s - best) * FACTOR)
            part = jnp.sum(e, axis=0, keepdims=True)
            values = jnp.concatenate(
                [values_of[t : t + 128] for t in range(lo, hi, 128)], axis=1
            )
            pv = jnp.dot(values, e.astype(BF16), preferred_element_type=F32)
            if not first:
                part = old[n][1] * alpha + part
                pv = old[n][2] * alpha + pv
            new.append((best, part, pv))
        for (best, part, pv), (h, qcols, qs, half, lo, hi) in zip(new, chains):
            if last:
                mine[qs, qcols] = (pv / part).T.astype(BF16)
            else:
                top[h, :, qs] = best
                total[h, :, qs] = part
                acc[h, :, qs] = pv

    def attend(d, g, first=False, last=False):
        def heads(r, carry):
            block_step(d, g, [r * HEADS_AT_ONCE + n for n in range(HEADS_AT_ONCE)], first, last)
            return carry

        lax.fori_loop(0, 4 // HEADS_AT_ONCE, heads, 0)

    out_cols = lambda g: pl.ds(pl.multiple_of(core * QCOLS + g * 512, 512), 512)

    def give(g):
        cols = slice(g * 512, g * 512 + 512)
        return copies.start(mine.at[other_rows, cols], out.at[:, out_cols(g)], partner)

    for n, d in ((0, 4), (0, 1)):
        arrived(n, d)
    attend(0, 0, first=True)
    for n, d in ((1, 4), (1, 1), (0, 3)):
        arrived(n, d)
    attend(0, 1, first=True)
    for n, d in ((2, 4), (2, 1), (1, 3)):
        arrived(n, d)
    attend(4, 0)
    for n, d in ((3, 4), (3, 1), (2, 3)):
        arrived(n, d)
    attend(1, 0)
    arrived(3, 3)
    attend(4, 1)
    attend(1, 1)
    attend(3, 0)
    attend(3, 1)
    arrived(0, 2)
    arrived(1, 2)
    attend(2, 0, last=True)
    back = [give(0)]
    arrived(2, 2)
    arrived(3, 2)
    attend(2, 1, last=True)
    back.append(give(1))
    for g in range(2):
        out[:, out_cols(g)] = mine[own_rows, g * 512 : g * 512 + 512]
    for copy in back:
        copy.wait_recv()
    copies.drain()
    for n in range(PIECES):
        for number in range(LEGS):
            do("wait", n, number)


def on_device(tokens, qkv_weight, route, offset, doc_lengths):
    half = HEAD_SIZE // 2
    freq = ROPE_BASE ** (-(jnp.arange(half, dtype=F32) * 2.0 / HEAD_SIZE))
    freq = jnp.concatenate([freq, freq])[None]
    vmem = pl.BlockSpec(memory_space=pltpu.VMEM)
    smem = pl.BlockSpec(memory_space=pltpu.SMEM)
    return pl.pallas_call(
        kernel,
        out_shape=jax.ShapeDtypeStruct((TOK, 2 * QCOLS), BF16),
        in_specs=[vmem, vmem, vmem, vmem, smem, vmem],
        out_specs=vmem,
        scratch_shapes=[
            pltpu.VMEM((N_DP, SLOT, MODEL), BF16),
            pltpu.VMEM((N_DP, 8, 128), I32),
            pltpu.VMEM((N_DP, SLOT, MODEL), BF16),
            pltpu.VMEM((N_DP, 8, 128), I32),
            pltpu.VMEM((N_DP, SLOT, MODEL), BF16),
            pltpu.VMEM((8, COLS), F32),
            pltpu.VMEM((8, COLS), F32),
            pltpu.VMEM((N_DP, CHIPS, 16, COLS), BF16),
            pltpu.VMEM((CHIP_TOK, MODEL), BF16),
            pltpu.VMEM((CHIP_TOK, HEAD_SIZE), F32),
            pltpu.VMEM((CHIP_TOK, HEAD_SIZE), F32),
            pltpu.VMEM((CHIP_TOK, QCOLS), BF16),
            pltpu.VMEM((PIECES, CHIP_TOK, HEAD_SIZE), BF16),
            pltpu.VMEM((REACH, PIECES, CHIP_TOK, HEAD_SIZE), BF16),
            pltpu.VMEM((CHIP_TOK, 128), BF16),
            pltpu.VMEM((REACH + 1, CHIP_TOK, 128), BF16),
            pltpu.VMEM((8, 1, CHIP_TOK), F32),
            pltpu.VMEM((8, 1, CHIP_TOK), F32),
            pltpu.VMEM((8, HEAD_SIZE, CHIP_TOK), F32),
            pltpu.VMEM((CHIP_TOK, QCOLS), BF16),
            pltpu.SemaphoreType.DMA((N_COPIES,)),
            pltpu.SemaphoreType.DMA((N_COPIES,)),
            pltpu.SemaphoreType.DMA((PIECES, LEGS)),
            pltpu.SemaphoreType.DMA((PIECES, REACH)),
        ],
        compiler_params=pltpu.CompilerParams(
            collective_id=0, has_side_effects=True, vmem_limit_bytes=50 * 2**20
        ),
    )(tokens, qkv_weight, route.reshape(1, TOK), offset.reshape(1, TOK), doc_lengths, freq)


def solution(mesh):
    in_specs = (
        P(("dp", "sp"), None),
        P(("dp", "sp"), None),
        P(("dp", "sp")),
        P(("dp", "sp")),
        P("dp", None),
    )
    out_specs = P(("dp", "sp"), None)
    return jax.shard_map(
        on_device, mesh=mesh, in_specs=in_specs, out_specs=out_specs, check_vma=False
    )
```

```python
import jax
import jax.numpy as jnp
from jax import lax
from jax.experimental import pallas as pl
from jax.experimental.pallas import tpu as pltpu
from jax.sharding import PartitionSpec as P

HEAD_SIZE = 128
ROPE_BASE = 500000.0
N_DP = 8
SIDE = 4
CHIPS = SIDE * SIDE
TOK = 256
CHIP_TOK = 2 * TOK
MODEL = 2048
SLOT = TOK // N_DP
QCOLS = 1024
KVCOLS = 256
COLS = QCOLS + 2 * KVCOLS
HALF = COLS // 2
REACH = 4
HEADS_AT_ONCE = 2
DOCS = 16
PIECES = 4
LEGS = 12
PASSING = 5
BIG = 2.0**100
FACTOR = HEAD_SIZE ** (-0.5) * 1.4426950408889634
EXTRA_RIGHT, EXTRA_LEFT = 4, 3
W_RIGHT, W_LEFT = 3, 4
ORDER = ((0, 0), (0, 1), (4, 0), (1, 0), (4, 1), (1, 1), (3, 0), (3, 1), (2, 0), (2, 1))
ARRIVALS = (
    ((), (), (), ()),
    ((), (), (), ()),
    (((0, 4), (2, 5), (1, 4), (3, 5),), ((0, 1), (0, 4), (1, 1), (1, 4),), ((0, 1), (0, 4), (1, 1), (1, 4),), ((0, 3), (0, 1), (0, 4), (1, 3), (1, 1), (1, 4),)),
    (((2, 4), (0, 3), (0, 1), (3, 4), (1, 3), (1, 1),), (), (), ()),
    (((2, 3),), ((2, 1), (2, 4), (0, 3), (3, 1), (3, 4),), ((2, 1), (2, 4), (0, 3), (3, 1), (3, 4),), ((2, 3), (2, 1), (2, 4), (3, 3), (3, 1), (3, 4),)),
    (((0, 2), (2, 1), (3, 3), (1, 2), (3, 1),), ((1, 3),), ((1, 3),), ()),
    ((), ((2, 3),), ((0, 2), (2, 2),), ((0, 2), (2, 2), (2, 5),)),
    (((2, 2),), ((0, 2), (3, 3),), ((1, 2), (2, 3), (3, 2), (3, 3),), ((1, 2), (3, 2), (3, 5),)),
    (((3, 2),), ((2, 2), (1, 2),), (), ()),
    ((), ((3, 2),), (), ()),
    ((), (), (), ()),
)
MESH = pl.DeviceIdType.MESH
F32 = jnp.float32
BF16 = jnp.bfloat16
I32 = jnp.int32


def iota(shape, dim):
    return lax.broadcasted_iota(I32, shape, dim)


class Copies:
    def __init__(self, send, recv):
        self.send, self.recv, self.made = send, recv, []

    def start(self, src, dst, device):
        n = len(self.made)
        copy = pltpu.make_async_remote_copy(
            src_ref=src,
            dst_ref=dst,
            send_sem=self.send.at[n],
            recv_sem=self.recv.at[n],
            device_id=device,
            device_id_type=MESH,
        )
        copy.start()
        self.made.append(copy)
        return copy

    def drain(self):
        for copy in self.made:
            copy.wait_send()


def greet(devices):
    barrier = pltpu.get_barrier_semaphore()
    for device in devices:
        pl.semaphore_signal(barrier, inc=1, device_id=device, device_id_type=MESH)
    return lambda: pl.semaphore_wait(barrier, len(devices))


N_COPIES = 1 + 7 + 7 + 2 * 7 + 2 * 2 * (4 + 16) + 4 + 2


def kernel(
    tokens_in, w_in, route_in, offset_in, lens, freq, out,
    tokens, w, route, offset,
    packed, ids, got, got_ids, extra, wsend, wrecv, wbuf, x,
    cosine, sine, q, kv, kvbuf, qdoc, kdoc, top, total, acc, mine,
    send, recv, leg_send, leg_recv, load,
):
    z = lax.axis_index("dp")
    sp = lax.axis_index("sp")
    core = lax.rem(sp, 2)
    chip = sp // 2
    cy, cx = chip // SIDE, lax.rem(chip, SIDE)
    partner = (z, sp + 1 - 2 * core)

    def at_z(d):
        return (lax.rem(z + d + N_DP, N_DP), sp)

    def place(dy, dx):
        return lax.rem(cy + dy + SIDE, SIDE) * SIDE + lax.rem(cx + dx + SIDE, SIDE)

    def at_chip(dy, dx):
        return (z, place(dy, dx) * 2 + core)

    def half_of(c):
        cols = lambda base, width: w[:, pl.ds(pl.multiple_of(base + c * width, 128), width)]
        return [
            (0, QCOLS, cols(0, QCOLS)),
            (QCOLS, KVCOLS, cols(2 * QCOLS, KVCOLS)),
            (QCOLS + KVCOLS, KVCOLS, cols(2 * QCOLS + 2 * KVCOLS, KVCOLS)),
        ]

    met = greet(
        [at_z(d) for d in range(1, N_DP)]
        + [partner]
        + [at_chip(0, 1), at_chip(0, -1), at_chip(1, 0), at_chip(-1, 0)]
    )
    loads = [
        pltpu.make_async_copy(here, there, load.at[n])
        for n, (here, there) in enumerate(
            [(w_in, w), (route_in, route), (offset_in, offset), (tokens_in, tokens)]
        )
    ]
    for copy in loads:
        copy.start()
    loads[0].wait()
    for base, width, part in half_of(1 - core):
        wsend[:, base : base + width] = part.astype(F32)

    met()
    copies = Copies(send, recv)

    swap = copies.start(wsend, wrecv, partner)

    for copy in loads[1:]:
        copy.wait()

    group = iota((8, TOK), 0)
    route_row = route[...]
    onehot = route_row == group
    before = (iota((TOK, TOK), 0) < iota((TOK, TOK), 1)).astype(F32).astype(BF16)
    rank = jnp.dot(
        onehot.astype(F32).astype(BF16), before, preferred_element_type=F32
    ).astype(I32)
    dest = jnp.where(rank < SLOT, group * SLOT + rank, N_DP * SLOT + rank - SLOT)
    dest = jnp.sum(jnp.where(onehot, dest, 0), axis=0, keepdims=True)

    def pack(block):
        pick = (iota((SLOT, TOK), 0) + block * SLOT == dest).astype(F32).astype(BF16)
        return jnp.dot(pick, tokens[...], preferred_element_type=F32).astype(BF16)

    def extra_ring(s):
        sent = []
        right, left = lax.rem(z - s + N_DP, N_DP), lax.rem(z + s, N_DP)
        if s < EXTRA_RIGHT:
            sent.append(copies.start(extra.at[right], extra.at[right], at_z(1)))
        if s < EXTRA_LEFT:
            sent.append(copies.start(extra.at[left], extra.at[left], at_z(-1)))
        return sent

    def w_ring(s):
        sent = []
        if s < W_RIGHT:
            here, there = (1 - s) % N_DP, -s % N_DP
            sent.append(copies.start(wbuf.at[here, chip], wbuf.at[there, chip], at_z(1)))
        if s < W_LEFT:
            sent.append(copies.start(wbuf.at[1 + s, chip], wbuf.at[2 + s, chip], at_z(-1)))
        return sent

    swap.wait_recv()
    for base, width, part in half_of(core):
        own = part.astype(F32)
        other = wrecv[:, base : base + width]
        first = jnp.where(core == 0, own, other)
        second = jnp.where(core == 0, other, own)
        wbuf[1, chip, :, base : base + width] = jnp.concatenate([first, second], axis=0).astype(BF16)
    w_tour = w_ring(0)

    facts = jnp.where(
        group == 0,
        offset[...] - sp * TOK,
        jnp.where(group == 1, route_row, jnp.where(group == 2, 1, 0)),
    ).astype(F32).astype(BF16)
    lane = iota((TOK, TOK), 0) - z * SLOT
    lane_ok = jnp.where((lane >= 0) & (lane < SLOT), lane, -10 * TOK)

    def numbers_of(block):
        pick = (lane_ok + block * SLOT == dest).astype(F32).astype(BF16)
        found = lax.dot_general(
            facts, pick, (((1,), (1,)), ((), ())), preferred_element_type=F32
        ).astype(I32)
        number = found[1:2] * TOK + found[0:1] + found[2:3]
        return [number[:, 0:128], number[:, 128:256]]

    extra[z] = pack(N_DP)
    more = numbers_of(N_DP) + [jnp.zeros((4, 128), I32)]

    def prepare(d):
        to = lax.rem(z + d, N_DP)
        packed[to] = pack(to)
        ids[to] = jnp.concatenate(numbers_of(to) + more, axis=0)

    def w_step(s):
        for copy in w_tour:
            copy.wait_recv()
        return w_ring(s)

    tokens_sent = []

    def send_tokens(d):
        to = lax.rem(z + d, N_DP)
        tokens_sent.append(copies.start(packed.at[to], got.at[z], at_z(d)))
        tokens_sent.append(copies.start(ids.at[to], got_ids.at[z], at_z(d)))

    def extra_step(s):
        for copy in tour:
            copy.wait_recv()
        return extra_ring(s)

    class Plane:
        def __init__(self, which, first, second, low, middle, high):
            self.which, self.first, self.second = which, first, second
            self.all, self.one, self.two = (low, high), (low, middle), (middle, high)

        def at(self, a, b):
            return (a * self.first[0] + b * self.second[0], a * self.first[1] + b * self.second[1])

        def send(self, a, b, blocks, to):
            ref = wbuf.at[
                pl.ds(blocks[0], blocks[1] - blocks[0]), place(*self.at(a, b)), :, pl.ds(self.which * HALF, HALF)
            ]
            return copies.start(ref, ref, at_chip(*self.at(*to)))

        def open(self):
            self.near = [self.send(0, 0, self.all, (1, 0)), self.send(0, 0, self.all, (-1, 0))]
            self.across = {}

        def spread(self, u):
            self.across[u] = [self.send(u, 0, self.all, (0, 1)), self.send(u, 0, self.all, (0, -1))]

        def forward(self):
            self.near[0].wait_recv()
            self.far = [self.send(-1, 0, self.one, (1, 0))]
            self.near[1].wait_recv()
            self.far.append(self.send(1, 0, self.two, (-1, 0)))

        def close(self):
            for copy in self.far:
                copy.wait_recv()

        def pass_on(self, u):
            self.across[u][0].wait_recv()
            one = self.send(u, -1, self.one, (0, 1))
            self.across[u][1].wait_recv()
            return [one, self.send(u, 1, self.two, (0, -1))]

    near, rest = (
        [Plane(0, (0, 1), (1, 0), *blocks), Plane(1, (1, 0), (0, 1), *blocks)]
        for blocks in ((0, 2, 3), (3, 5, 8))
    )
    last = []

    def open_plane(planes):
        for plane in planes:
            plane.open()
        for plane in planes:
            plane.spread(0)

    def widen(planes):
        for plane in planes:
            plane.forward()
        for plane in planes:
            plane.spread(-1)
            plane.spread(1)

    def finish(planes):
        for plane in planes:
            plane.close()
            plane.spread(2)

    def pass_on(planes, u):
        for plane in planes:
            last.extend(plane.pass_on(u))

    tour = extra_ring(0)
    for d in (1, 7):
        prepare(d)
        send_tokens(d)
    w_tour = w_step(1)
    open_plane(near)
    for d in (3, 2):
        prepare(d)
    tour = extra_step(1)
    widen(near)
    w_tour = w_step(2)
    tour = extra_step(2)
    send_tokens(3)
    for d in (5, 6, 4):
        prepare(d)
    finish(near)
    pass_on(near, 0)
    w_tour = w_step(3)
    send_tokens(5)
    send_tokens(2)
    pass_on(near, -1)
    tour = extra_step(3)
    send_tokens(6)
    send_tokens(4)
    pass_on(near, 1)
    w_tour = w_step(4)
    open_plane(rest)
    pass_on(near, 2)
    prepare(0)
    got[z] = packed[z]
    got_ids[z] = ids[z]

    lanes = iota((1, 128), 1)
    starts = jnp.full((1, 128), 2**30, I32)
    ends = jnp.full((1, 128), 2**30, I32)
    row = iota((CHIP_TOK, 128), 0) + chip * CHIP_TOK
    begin_of = jnp.zeros((CHIP_TOK, 128), I32)
    begin = lens[0, 0] * 0
    for e in range(DOCS):
        starts = jnp.where(lanes == e, begin, starts)
        begin_of = jnp.where(row >= begin, begin, begin_of)
        begin = begin + lens[0, e]
        ends = jnp.where(lanes == e, begin, ends)
    angle = (row - begin_of).astype(F32) * freq[...]
    cosine[...] = jnp.cos(angle)
    sine[...] = jnp.sin(angle) * jnp.where(lanes < 64, -1.0, 1.0)

    def member(base):
        point = iota((CHIP_TOK, 128), 0) + base
        return (point >= starts) & (point < ends)

    qdoc[...] = jnp.where(member(chip * CHIP_TOK), 1.0, 0.0).astype(BF16)
    for d in range(REACH + 1):
        kdoc[d] = jnp.where(member((chip - d) * CHIP_TOK), 0.0, -BIG).astype(BF16)

    widen(rest)
    finish(rest)
    pass_on(rest, 0)
    tour = extra_step(4)
    for u in (-1, 1, 2):
        pass_on(rest, u)

    for copy in tokens_sent:
        copy.wait_recv()
    mine_ids = iota((TOK, TOK), 0) + z * TOK + 1
    numbers = jnp.zeros((8, 128), I32)
    for source in range(N_DP):
        numbers += got_ids[source]
    to_place = [
        (jnp.concatenate([numbers[n : n + 1], numbers[n + 1 : n + 2]], axis=1) == mine_ids)
        .astype(F32)
        .astype(BF16)
        for n in (0, 2)
    ]
    own_rows = pl.ds(pl.multiple_of(core * TOK, TOK), TOK)
    other_rows = pl.ds(pl.multiple_of((1 - core) * TOK, TOK), TOK)
    shared = []
    for part in range(N_DP):
        from_z = lax.rem(z + part + N_DP - 1, N_DP)
        cols = pl.ds(pl.multiple_of(from_z * 256, 256), 256)
        rows = jnp.dot(
            to_place[0], got[:, :, cols].reshape(TOK, 256), preferred_element_type=F32
        ) + jnp.dot(
            to_place[1], extra[:, :, cols].reshape(TOK, 256), preferred_element_type=F32
        )
        x[own_rows, part * 256 : part * 256 + 256] = rows.astype(BF16)
        if part % 2:
            ready = x.at[own_rows, part * 256 - 256 : part * 256 + 256]
            shared.append(copies.start(ready, ready, partner))
    for copy in last:
        copy.wait_recv()

    def project(c, rows):
        cols = pl.ds(pl.multiple_of(c * 256, 256), 256)
        weights = wbuf[:, :, :, cols].reshape(MODEL, 256)
        return jnp.dot(x[rows], weights, preferred_element_type=F32).astype(BF16)

    def rotated(y, rows):
        parts = []
        for n in range(2):
            v = y[:, n * 128 : n * 128 + 128].astype(F32)
            parts.append((v * cosine[rows] + pltpu.roll(v, 64, 1) * sine[rows]).astype(BF16))
        return parts

    def project_keys(rows, base):
        keys = rotated(project(4, rows), rows)
        values = project(5, rows).astype(F32)
        for g in range(2):
            kv[2 * g, rows] = keys[g]
            for t in range(2):
                block = values[t * 128 : t * 128 + 128, g * 128 : g * 128 + 128]
                at = pl.ds(pl.multiple_of(base + t * 128, 128), 128)
                kv[2 * g + 1, at] = block.T.astype(BF16)

    project_keys(own_rows, core * TOK)
    for copy in shared:
        copy.wait_recv()
    project_keys(other_rows, (1 - core) * TOK)

    def leg(n, number, d, to, source, when):
        copy = pltpu.make_async_remote_copy(
            src_ref=source,
            dst_ref=kvbuf.at[d - 1, n],
            send_sem=leg_send.at[n, number],
            recv_sem=leg_recv.at[n, d - 1],
            device_id=to,
            device_id_type=MESH,
        )
        return copy, when

    def legs(n):
        own, came = kv.at[n], lambda d: kvbuf.at[d - 1, n]
        right, left, down = at_chip(0, 1), at_chip(0, -1), at_chip(1, 0)
        inner = (cx == 1) | (cx == 2)
        first = [(4, down, own, None), (1, right, own, cx < 3), (3, left, own, cx == 0)]
        if n < 2:
            return {
                0: first,
                4: [(3, left, came(4), cx > 0), (1, right, came(4), cx == 3)],
                1: [(2, right, came(1), inner)],
                3: [(2, left, came(3), inner)],
            }
        return {
            0: first + [(PASSING, left, own, cx == 1)],
            4: [(3, left, came(4), cx > 1), (1, right, came(4), cx == 3)],
            1: [(2, right, came(1), cx == 0), (PASSING, down, came(1), cx == 3)],
            PASSING: [
                (2, left, came(PASSING), cx == 0),
                (3, down, came(PASSING), cx == 0),
                (2, right, came(PASSING), cx == 3),
            ],
            3: [(2, left, came(3), cx == 3)],
        }

    routes, number = [], 0
    for n in range(PIECES):
        number = 0
        route_of = {}
        for cause, parts in legs(n).items():
            route_of[cause] = []
            for d, to, source, when in parts:
                route_of[cause].append(leg(n, number, d, to, source, when))
                number += 1
        routes.append(route_of)

    def do(action, n, cause):
        for copy, when in routes[n].get(cause, []):
            run = copy.start if action == "start" else copy.wait_send
            if when is None:
                run()
            else:
                pl.when(when)(run)

    def arrived(n, d):
        wait = pltpu.make_async_remote_copy(
            src_ref=kvbuf.at[d - 1, n],
            dst_ref=kvbuf.at[d - 1, n],
            send_sem=leg_send.at[n, 0],
            recv_sem=leg_recv.at[n, d - 1],
            device_id=partner,
            device_id_type=MESH,
        ).wait_recv
        wait()
        do("start", n, d)

    for n in range(PIECES):
        do("start", n, 0)

    def query(c, carry):
        for n, part in enumerate(rotated(project(c, slice(0, CHIP_TOK)), slice(0, CHIP_TOK))):
            q[:, pl.ds(pl.multiple_of(c * 256 + n * 128, 128), 128)] = part
        return carry

    lax.fori_loop(0, 4, query, 0)

    def block_step(d, g, heads, first, last):
        keys_of = kv.at[2 * g] if d == 0 else kvbuf.at[d - 1, 2 * g]
        values_of = kv.at[2 * g + 1] if d == 0 else kvbuf.at[d - 1, 2 * g + 1]
        chains = []
        for r in heads:
            h = g * 4 + r
            qcols = pl.ds(pl.multiple_of(h * 128, 128), 128)
            for half in range(2):
                lo, hi = 0, 512
                if d == 0 and half == 0:
                    hi = 256
                if d == REACH and half == 1:
                    lo = 256
                chains.append((h, qcols, slice(half * 256, half * 256 + 256), half, lo, hi))
        scores, old = [], []
        for h, qcols, qs, half, lo, hi in chains:
            keys = jnp.concatenate([keys_of[lo:hi], kdoc[d, lo:hi]], axis=1)
            query = jnp.concatenate([q[qs, qcols], qdoc[qs]], axis=1)
            s = lax.dot_general(
                keys, query, (((1,), (1,)), ((), ())), preferred_element_type=F32
            )
            if d == 0:
                n = hi - lo
                seen = iota((n, 256), 0) + lo <= iota((n, 256), 1) + half * 256
                s = jnp.where(seen, s, -BIG)
            scores.append(s)
            if not first:
                old.append((top[h, :, qs], total[h, :, qs], acc[h, :, qs]))
        new = []
        for n, (h, qcols, qs, half, lo, hi) in enumerate(chains):
            s = scores[n]
            best = jnp.max(s, axis=0, keepdims=True)
            if not first:
                best = jnp.maximum(old[n][0], best)
                alpha = jnp.exp2((old[n][0] - best) * FACTOR)
            e = jnp.exp2((s - best) * FACTOR)
            part = jnp.sum(e, axis=0, keepdims=True)
            values = jnp.concatenate(
                [values_of[t : t + 128] for t in range(lo, hi, 128)], axis=1
            )
            pv = jnp.dot(values, e.astype(BF16), preferred_element_type=F32)
            if not first:
                part = old[n][1] * alpha + part
                pv = old[n][2] * alpha + pv
            new.append((best, part, pv))
        for (best, part, pv), (h, qcols, qs, half, lo, hi) in zip(new, chains):
            if last:
                mine[qs, qcols] = (pv / part).T.astype(BF16)
            else:
                top[h, :, qs] = best
                total[h, :, qs] = part
                acc[h, :, qs] = pv

    def attend(d, g, first=False, last=False):
        def heads(r, carry):
            block_step(d, g, [r * HEADS_AT_ONCE + n for n in range(HEADS_AT_ONCE)], first, last)
            return carry

        lax.fori_loop(0, 4 // HEADS_AT_ONCE, heads, 0)

    out_cols = lambda g: pl.ds(pl.multiple_of(core * QCOLS + g * 512, 512), 512)

    def give(g):
        cols = slice(g * 512, g * 512 + 512)
        return copies.start(mine.at[other_rows, cols], out.at[:, out_cols(g)], partner)

    def arrive(step):
        for column, events in enumerate(ARRIVALS[step]):
            if events:

                @pl.when(cx == column)
                def _(events=events):
                    for n, d in events:
                        arrived(n, d)

    back = []
    for step, (d, g) in enumerate(ORDER):
        arrive(step)
        attend(d, g, first=d == 0, last=d == 2)
        if d == 2:
            back.append(give(g))
    for g in range(2):
        out[:, out_cols(g)] = mine[own_rows, g * 512 : g * 512 + 512]
    arrive(len(ORDER))
    for copy in back:
        copy.wait_recv()
    copies.drain()
    for n in range(PIECES):
        for cause in routes[n]:
            do("wait", n, cause)


def on_device(tokens, qkv_weight, route, offset, doc_lengths):
    half = HEAD_SIZE // 2
    freq = ROPE_BASE ** (-(jnp.arange(half, dtype=F32) * 2.0 / HEAD_SIZE))
    freq = jnp.concatenate([freq, freq])[None]
    vmem = pl.BlockSpec(memory_space=pltpu.VMEM)
    hbm = pl.BlockSpec(memory_space=pltpu.HBM)
    smem = pl.BlockSpec(memory_space=pltpu.SMEM)
    return pl.pallas_call(
        kernel,
        out_shape=jax.ShapeDtypeStruct((TOK, 2 * QCOLS), BF16),
        in_specs=[hbm, hbm, hbm, hbm, smem, vmem],
        out_specs=vmem,
        scratch_shapes=[
            pltpu.VMEM((TOK, MODEL), BF16),
            pltpu.VMEM((8, 2 * COLS), BF16),
            pltpu.VMEM((1, TOK), I32),
            pltpu.VMEM((1, TOK), I32),
            pltpu.VMEM((N_DP, SLOT, MODEL), BF16),
            pltpu.VMEM((N_DP, 8, 128), I32),
            pltpu.VMEM((N_DP, SLOT, MODEL), BF16),
            pltpu.VMEM((N_DP, 8, 128), I32),
            pltpu.VMEM((N_DP, SLOT, MODEL), BF16),
            pltpu.VMEM((8, COLS), F32),
            pltpu.VMEM((8, COLS), F32),
            pltpu.VMEM((N_DP, CHIPS, 16, COLS), BF16),
            pltpu.VMEM((CHIP_TOK, MODEL), BF16),
            pltpu.VMEM((CHIP_TOK, HEAD_SIZE), F32),
            pltpu.VMEM((CHIP_TOK, HEAD_SIZE), F32),
            pltpu.VMEM((CHIP_TOK, QCOLS), BF16),
            pltpu.VMEM((PIECES, CHIP_TOK, HEAD_SIZE), BF16),
            pltpu.VMEM((PASSING, PIECES, CHIP_TOK, HEAD_SIZE), BF16),
            pltpu.VMEM((CHIP_TOK, 128), BF16),
            pltpu.VMEM((REACH + 1, CHIP_TOK, 128), BF16),
            pltpu.VMEM((8, 1, CHIP_TOK), F32),
            pltpu.VMEM((8, 1, CHIP_TOK), F32),
            pltpu.VMEM((8, HEAD_SIZE, CHIP_TOK), F32),
            pltpu.VMEM((CHIP_TOK, QCOLS), BF16),
            pltpu.SemaphoreType.DMA((N_COPIES,)),
            pltpu.SemaphoreType.DMA((N_COPIES,)),
            pltpu.SemaphoreType.DMA((PIECES, LEGS)),
            pltpu.SemaphoreType.DMA((PIECES, PASSING)),
            pltpu.SemaphoreType.DMA((4,)),
        ],
        compiler_params=pltpu.CompilerParams(
            collective_id=0, has_side_effects=True, vmem_limit_bytes=50 * 2**20
        ),
    )(tokens, qkv_weight, route.reshape(1, TOK), offset.reshape(1, TOK), doc_lengths, freq)


def solution(mesh):
    in_specs = (
        P(("dp", "sp"), None),
        P(("dp", "sp"), None),
        P(("dp", "sp")),
        P(("dp", "sp")),
        P("dp", None),
    )
    out_specs = P(("dp", "sp"), None)
    return jax.shard_map(
        on_device, mesh=mesh, in_specs=in_specs, out_specs=out_specs, check_vma=False
    )
```

```python
import jax
import jax.numpy as jnp
from jax import lax
from jax.experimental import pallas as pl
from jax.experimental.pallas import tpu as pltpu
from jax.sharding import PartitionSpec as P

HEAD_SIZE = 128
ROPE_BASE = 500000.0
N_DP = 8
SIDE = 4
CHIPS = SIDE * SIDE
TOK = 256
CHIP_TOK = 2 * TOK
MODEL = 2048
SLOT = TOK // N_DP
QCOLS = 1024
KVCOLS = 256
COLS = QCOLS + 2 * KVCOLS
HALF = COLS // 2
REACH = 4
HEADS_AT_ONCE = 4
DOCS = 16
PIECES = 8
CROSSING = (2, 5, 7)
LEGS = 12
PASSING = 5
BIG = 2.0**100
FACTOR = HEAD_SIZE ** (-0.5) * 1.4426950408889634
EXTRA_RIGHT, EXTRA_LEFT = 4, 3
W_RIGHT, W_LEFT = 3, 4
ORDER = ((0, 0), (0, 1), (4, 0), (1, 0), (4, 1), (1, 1), (3, 0), (3, 1), (2, 0), (2, 1))
ARRIVALS = (
    ((), (), (), ()),
    ((), (), (), ()),
    (((0, 4), (2, 5), (1, 4), (5, 5), (2, 4), (7, 5), (3, 4),), ((0, 1), (0, 4), (1, 1), (1, 4), (2, 1), (2, 4), (3, 1), (3, 4),), ((0, 1), (0, 4), (1, 1), (1, 4), (2, 1), (2, 4), (3, 1), (3, 4),), ((0, 3), (0, 1), (0, 4), (1, 3), (1, 1), (1, 4), (2, 3), (2, 1), (2, 4), (3, 3), (3, 1), (3, 4),)),
    (((0, 3), (0, 1), (4, 4), (1, 3), (1, 1), (5, 4), (2, 1), (3, 3), (6, 4), (3, 1),), ((0, 3), (4, 1), (4, 4), (1, 3),), ((0, 3), (4, 1), (4, 4), (1, 3),), ((4, 3), (4, 1), (4, 4),)),
    (((0, 2), (7, 4), (4, 1), (4, 3),), ((5, 1), (5, 4), (2, 3), (6, 1), (6, 4), (3, 3), (7, 1), (7, 4),), ((5, 1), (5, 4), (2, 2), (6, 1), (6, 4), (2, 3), (7, 1), (7, 4),), ((5, 3), (5, 1), (5, 4), (6, 3), (6, 1), (6, 4), (7, 3), (7, 1), (7, 4),)),
    (((2, 3), (5, 1), (1, 2), (5, 3), (6, 1), (6, 3), (7, 3), (7, 1),), ((0, 2), (2, 2), (4, 3),), ((3, 3), (0, 2),), ((0, 2), (2, 2), (2, 5),)),
    (((3, 2), (2, 2), (4, 2),), ((1, 2),), ((4, 3), (1, 2), (5, 2),), ((1, 2), (5, 2), (5, 5),)),
    (((5, 2),), ((5, 3), (6, 3), (5, 2), (7, 3),), ((3, 2), (5, 3), (4, 2), (6, 3), (6, 2), (7, 2), (7, 3),), ((7, 2), (3, 2), (7, 5), (4, 2),)),
    (((7, 2), (6, 2),), ((7, 2), (3, 2),), (), ((6, 2),)),
    ((), ((4, 2), (6, 2),), (), ()),
    ((), (), (), ()),
)
MESH = pl.DeviceIdType.MESH
F32 = jnp.float32
BF16 = jnp.bfloat16
I32 = jnp.int32


def iota(shape, dim):
    return lax.broadcasted_iota(I32, shape, dim)


class Copies:
    def __init__(self, send, recv):
        self.send, self.recv, self.made = send, recv, []

    def start(self, src, dst, device):
        n = len(self.made)
        copy = pltpu.make_async_remote_copy(
            src_ref=src,
            dst_ref=dst,
            send_sem=self.send.at[n],
            recv_sem=self.recv.at[n],
            device_id=device,
            device_id_type=MESH,
        )
        copy.start()
        self.made.append(copy)
        return copy

    def drain(self):
        for copy in self.made:
            copy.wait_send()


def greet(devices):
    barrier = pltpu.get_barrier_semaphore()
    for device in devices:
        pl.semaphore_signal(barrier, inc=1, device_id=device, device_id_type=MESH)
    return lambda: pl.semaphore_wait(barrier, len(devices))


N_COPIES = 1 + 7 + 7 + 2 * 7 + 2 * 2 * (4 + 16) + 4 + 2


def kernel(
    tokens_in, w_in, route_in, offset_in, lens, freq, out,
    tokens, w, route, offset,
    packed, ids, got, got_ids, extra, wsend, wrecv, wbuf, x,
    cosine, sine, q, kv, kvbuf, qdoc, kdoc, top, total, acc, mine,
    send, recv, leg_send, leg_recv, load,
):
    z = lax.axis_index("dp")
    sp = lax.axis_index("sp")
    core = lax.rem(sp, 2)
    chip = sp // 2
    cy, cx = chip // SIDE, lax.rem(chip, SIDE)
    partner = (z, sp + 1 - 2 * core)

    def at_z(d):
        return (lax.rem(z + d + N_DP, N_DP), sp)

    def place(dy, dx):
        return lax.rem(cy + dy + SIDE, SIDE) * SIDE + lax.rem(cx + dx + SIDE, SIDE)

    def at_chip(dy, dx):
        return (z, place(dy, dx) * 2 + core)

    def half_of(c):
        cols = lambda base, width: w[:, pl.ds(pl.multiple_of(base + c * width, 128), width)]
        return [
            (0, QCOLS, cols(0, QCOLS)),
            (QCOLS, KVCOLS, cols(2 * QCOLS, KVCOLS)),
            (QCOLS + KVCOLS, KVCOLS, cols(2 * QCOLS + 2 * KVCOLS, KVCOLS)),
        ]

    met = greet(
        [at_z(d) for d in range(1, N_DP)]
        + [partner]
        + [at_chip(0, 1), at_chip(0, -1), at_chip(1, 0), at_chip(-1, 0)]
    )
    loads = [
        pltpu.make_async_copy(here, there, load.at[n])
        for n, (here, there) in enumerate(
            [(w_in, w), (route_in, route), (offset_in, offset), (tokens_in, tokens)]
        )
    ]
    for copy in loads:
        copy.start()
    loads[0].wait()
    for base, width, part in half_of(1 - core):
        wsend[:, base : base + width] = part.astype(F32)

    met()
    copies = Copies(send, recv)

    swap = copies.start(wsend, wrecv, partner)

    for copy in loads[1:]:
        copy.wait()

    group = iota((8, TOK), 0)
    route_row = route[...]
    onehot = route_row == group
    before = (iota((TOK, TOK), 0) < iota((TOK, TOK), 1)).astype(F32).astype(BF16)
    rank = jnp.dot(
        onehot.astype(F32).astype(BF16), before, preferred_element_type=F32
    ).astype(I32)
    dest = jnp.where(rank < SLOT, group * SLOT + rank, N_DP * SLOT + rank - SLOT)
    dest = jnp.sum(jnp.where(onehot, dest, 0), axis=0, keepdims=True)

    def pack(block):
        pick = (iota((SLOT, TOK), 0) + block * SLOT == dest).astype(F32).astype(BF16)
        return jnp.dot(pick, tokens[...], preferred_element_type=F32).astype(BF16)

    def extra_ring(s):
        sent = []
        right, left = lax.rem(z - s + N_DP, N_DP), lax.rem(z + s, N_DP)
        if s < EXTRA_RIGHT:
            sent.append(copies.start(extra.at[right], extra.at[right], at_z(1)))
        if s < EXTRA_LEFT:
            sent.append(copies.start(extra.at[left], extra.at[left], at_z(-1)))
        return sent

    def w_ring(s):
        sent = []
        if s < W_RIGHT:
            here, there = (1 - s) % N_DP, -s % N_DP
            sent.append(copies.start(wbuf.at[here, chip], wbuf.at[there, chip], at_z(1)))
        if s < W_LEFT:
            sent.append(copies.start(wbuf.at[1 + s, chip], wbuf.at[2 + s, chip], at_z(-1)))
        return sent

    facts = jnp.where(
        group == 0,
        offset[...] - sp * TOK,
        jnp.where(group == 1, route_row, jnp.where(group == 2, 1, 0)),
    ).astype(F32).astype(BF16)
    lane = iota((TOK, TOK), 0) - z * SLOT
    lane_ok = jnp.where((lane >= 0) & (lane < SLOT), lane, -10 * TOK)

    def numbers_of(block):
        pick = (lane_ok + block * SLOT == dest).astype(F32).astype(BF16)
        found = lax.dot_general(
            facts, pick, (((1,), (1,)), ((), ())), preferred_element_type=F32
        ).astype(I32)
        number = found[1:2] * TOK + found[0:1] + found[2:3]
        return [number[:, 0:128], number[:, 128:256]]

    more = numbers_of(N_DP) + [jnp.zeros((4, 128), I32)]

    def prepare(d):
        to = lax.rem(z + d, N_DP)
        packed[to] = pack(to)
        ids[to] = jnp.concatenate(numbers_of(to) + more, axis=0)

    tokens_sent = []

    def send_tokens(d):
        to = lax.rem(z + d, N_DP)
        tokens_sent.append(copies.start(packed.at[to], got.at[z], at_z(d)))
        tokens_sent.append(copies.start(ids.at[to], got_ids.at[z], at_z(d)))

    for d in (1, 7):
        prepare(d)
        send_tokens(d)

    swap.wait_recv()
    for base, width, part in half_of(core):
        own = part.astype(F32)
        other = wrecv[:, base : base + width]
        first = jnp.where(core == 0, own, other)
        second = jnp.where(core == 0, other, own)
        wbuf[1, chip, :, base : base + width] = jnp.concatenate([first, second], axis=0).astype(BF16)
    w_tour = w_ring(0)

    extra[z] = pack(N_DP)
    tour = extra_ring(0)

    def w_step(s):
        for copy in w_tour:
            copy.wait_recv()
        return w_ring(s)

    def extra_step(s):
        for copy in tour:
            copy.wait_recv()
        return extra_ring(s)

    class Plane:
        def __init__(self, which, first, second, low, middle, high):
            self.which, self.first, self.second = which, first, second
            self.all, self.one, self.two = (low, high), (low, middle), (middle, high)

        def at(self, a, b):
            return (a * self.first[0] + b * self.second[0], a * self.first[1] + b * self.second[1])

        def send(self, a, b, blocks, to):
            ref = wbuf.at[
                pl.ds(blocks[0], blocks[1] - blocks[0]), place(*self.at(a, b)), :, pl.ds(self.which * HALF, HALF)
            ]
            return copies.start(ref, ref, at_chip(*self.at(*to)))

        def open(self):
            self.near = [self.send(0, 0, self.all, (1, 0)), self.send(0, 0, self.all, (-1, 0))]
            self.across = {}

        def spread(self, u):
            self.across[u] = [self.send(u, 0, self.all, (0, 1)), self.send(u, 0, self.all, (0, -1))]

        def forward(self):
            self.near[0].wait_recv()
            self.far = [self.send(-1, 0, self.one, (1, 0))]
            self.near[1].wait_recv()
            self.far.append(self.send(1, 0, self.two, (-1, 0)))

        def close(self):
            for copy in self.far:
                copy.wait_recv()

        def pass_on(self, u):
            self.across[u][0].wait_recv()
            one = self.send(u, -1, self.one, (0, 1))
            self.across[u][1].wait_recv()
            return [one, self.send(u, 1, self.two, (0, -1))]

    near, rest = (
        [Plane(0, (0, 1), (1, 0), *blocks), Plane(1, (1, 0), (0, 1), *blocks)]
        for blocks in ((0, 2, 3), (3, 5, 8))
    )
    last = []

    def open_plane(planes):
        for plane in planes:
            plane.open()
        for plane in planes:
            plane.spread(0)

    def widen(planes):
        for plane in planes:
            plane.forward()
        for plane in planes:
            plane.spread(-1)
            plane.spread(1)

    def finish(planes):
        for plane in planes:
            plane.close()
            plane.spread(2)

    def pass_on(planes, u):
        for plane in planes:
            last.extend(plane.pass_on(u))

    w_tour = w_step(1)
    open_plane(near)
    for d in (3, 2):
        prepare(d)
    tour = extra_step(1)
    widen(near)
    w_tour = w_step(2)
    tour = extra_step(2)
    send_tokens(3)
    for d in (5, 6, 4):
        prepare(d)
    finish(near)
    pass_on(near, 0)
    w_tour = w_step(3)
    send_tokens(5)
    send_tokens(2)
    pass_on(near, -1)
    tour = extra_step(3)
    send_tokens(6)
    send_tokens(4)
    pass_on(near, 1)
    w_tour = w_step(4)
    open_plane(rest)
    pass_on(near, 2)
    prepare(0)
    got[z] = packed[z]
    got_ids[z] = ids[z]

    lanes = iota((1, 128), 1)
    starts = jnp.full((1, 128), 2**30, I32)
    ends = jnp.full((1, 128), 2**30, I32)
    row = iota((CHIP_TOK, 128), 0) + chip * CHIP_TOK
    begin_of = jnp.zeros((CHIP_TOK, 128), I32)
    begin = lens[0, 0] * 0
    for e in range(DOCS):
        starts = jnp.where(lanes == e, begin, starts)
        begin_of = jnp.where(row >= begin, begin, begin_of)
        begin = begin + lens[0, e]
        ends = jnp.where(lanes == e, begin, ends)
    angle = (row - begin_of).astype(F32) * freq[...]
    cosine[...] = jnp.cos(angle)
    sine[...] = jnp.sin(angle) * jnp.where(lanes < 64, -1.0, 1.0)

    def member(base):
        point = iota((CHIP_TOK, 128), 0) + base
        return (point >= starts) & (point < ends)

    qdoc[...] = jnp.where(member(chip * CHIP_TOK), 1.0, 0.0).astype(BF16)
    for d in range(REACH + 1):
        kdoc[d] = jnp.where(member((chip - d) * CHIP_TOK), 0.0, -BIG).astype(BF16)

    widen(rest)
    finish(rest)
    pass_on(rest, 0)
    tour = extra_step(4)
    for u in (-1, 1, 2):
        pass_on(rest, u)

    for copy in tokens_sent:
        copy.wait_recv()
    mine_ids = iota((TOK, TOK), 0) + z * TOK + 1
    numbers = jnp.zeros((8, 128), I32)
    for source in range(N_DP):
        numbers += got_ids[source]
    to_place = [
        (jnp.concatenate([numbers[n : n + 1], numbers[n + 1 : n + 2]], axis=1) == mine_ids)
        .astype(F32)
        .astype(BF16)
        for n in (0, 2)
    ]
    own_rows = pl.ds(pl.multiple_of(core * TOK, TOK), TOK)
    other_rows = pl.ds(pl.multiple_of((1 - core) * TOK, TOK), TOK)
    shared = []
    for part in range(N_DP):
        from_z = lax.rem(z + part + N_DP - 1, N_DP)
        cols = pl.ds(pl.multiple_of(from_z * 256, 256), 256)
        rows = jnp.dot(
            to_place[0], got[:, :, cols].reshape(TOK, 256), preferred_element_type=F32
        ) + jnp.dot(
            to_place[1], extra[:, :, cols].reshape(TOK, 256), preferred_element_type=F32
        )
        x[own_rows, part * 256 : part * 256 + 256] = rows.astype(BF16)
        if part % 2:
            ready = x.at[own_rows, part * 256 - 256 : part * 256 + 256]
            shared.append(copies.start(ready, ready, partner))
    for copy in last:
        copy.wait_recv()

    def project(c, rows):
        cols = pl.ds(pl.multiple_of(c * 256, 256), 256)
        weights = wbuf[:, :, :, cols].reshape(MODEL, 256)
        return jnp.dot(x[rows], weights, preferred_element_type=F32).astype(BF16)

    def rotated(y, rows):
        parts = []
        for n in range(2):
            v = y[:, n * 128 : n * 128 + 128].astype(F32)
            parts.append((v * cosine[rows] + pltpu.roll(v, 64, 1) * sine[rows]).astype(BF16))
        return parts

    def project_keys(rows, base):
        keys = rotated(project(4, rows), rows)
        values = project(5, rows).astype(F32)
        for g in range(2):
            kv[2 * g, rows] = keys[g]
            for t in range(2):
                block = values[t * 128 : t * 128 + 128, g * 128 : g * 128 + 128]
                at = pl.ds(pl.multiple_of(base + t * 128, 128), 128)
                kv[2 * g + 1, at] = block.T.astype(BF16)

    def queries(rows):
        def query(c, carry):
            for n, part in enumerate(rotated(project(c, rows), rows)):
                q[rows, pl.ds(pl.multiple_of(c * 256 + n * 128, 128), 128)] = part
            return carry

        lax.fori_loop(0, 4, query, 0)

    project_keys(own_rows, core * TOK)
    queries(own_rows)
    for copy in shared:
        copy.wait_recv()
    project_keys(other_rows, (1 - core) * TOK)

    def piece(n):
        return n // 2, slice(n % 2 * 256, n % 2 * 256 + 256)

    def leg(n, number, d, to, source, when):
        copy = pltpu.make_async_remote_copy(
            src_ref=source,
            dst_ref=kvbuf.at[(d - 1, *piece(n))],
            send_sem=leg_send.at[n, number],
            recv_sem=leg_recv.at[n, d - 1],
            device_id=to,
            device_id_type=MESH,
        )
        return copy, when

    def legs(n):
        own, came = kv.at[piece(n)], lambda d: kvbuf.at[(d - 1, *piece(n))]
        right, left, down = at_chip(0, 1), at_chip(0, -1), at_chip(1, 0)
        inner = (cx == 1) | (cx == 2)
        first = [(4, down, own, None), (1, right, own, cx < 3), (3, left, own, cx == 0)]
        if n not in CROSSING:
            return {
                0: first,
                4: [(3, left, came(4), cx > 0), (1, right, came(4), cx == 3)],
                1: [(2, right, came(1), inner)],
                3: [(2, left, came(3), inner)],
            }
        return {
            0: first + [(PASSING, left, own, cx == 1)],
            4: [(3, left, came(4), cx > 1), (1, right, came(4), cx == 3)],
            1: [(2, right, came(1), cx == 0), (PASSING, down, came(1), cx == 3)],
            PASSING: [
                (2, left, came(PASSING), cx == 0),
                (3, down, came(PASSING), cx == 0),
                (2, right, came(PASSING), cx == 3),
            ],
            3: [(2, left, came(3), cx == 3)],
        }

    routes, number = [], 0
    for n in range(PIECES):
        number = 0
        route_of = {}
        for cause, parts in legs(n).items():
            route_of[cause] = []
            for d, to, source, when in parts:
                route_of[cause].append(leg(n, number, d, to, source, when))
                number += 1
        routes.append(route_of)

    def do(action, n, cause):
        for copy, when in routes[n].get(cause, []):
            run = copy.start if action == "start" else copy.wait_send
            if when is None:
                run()
            else:
                pl.when(when)(run)

    def arrived(n, d):
        wait = pltpu.make_async_remote_copy(
            src_ref=kvbuf.at[(d - 1, *piece(n))],
            dst_ref=kvbuf.at[(d - 1, *piece(n))],
            send_sem=leg_send.at[n, 0],
            recv_sem=leg_recv.at[n, d - 1],
            device_id=partner,
            device_id_type=MESH,
        ).wait_recv
        wait()
        do("start", n, d)

    for n in range(PIECES):
        do("start", n, 0)

    queries(other_rows)

    def block_step(d, g, heads, first, last):
        keys_of = kv.at[2 * g] if d == 0 else kvbuf.at[d - 1, 2 * g]
        values_of = kv.at[2 * g + 1] if d == 0 else kvbuf.at[d - 1, 2 * g + 1]
        chains = []
        for r in heads:
            h = g * 4 + r
            qcols = pl.ds(pl.multiple_of(h * 128, 128), 128)
            for half in range(2):
                lo, hi = 0, 512
                if d == 0 and half == 0:
                    hi = 256
                if d == REACH and half == 1:
                    lo = 256
                chains.append((h, qcols, slice(half * 256, half * 256 + 256), half, lo, hi))
        scores, old = [], []
        for h, qcols, qs, half, lo, hi in chains:
            keys = jnp.concatenate([keys_of[lo:hi], kdoc[d, lo:hi]], axis=1)
            query = jnp.concatenate([q[qs, qcols], qdoc[qs]], axis=1)
            s = lax.dot_general(
                keys, query, (((1,), (1,)), ((), ())), preferred_element_type=F32
            )
            if d == 0:
                n = hi - lo
                seen = iota((n, 256), 0) + lo <= iota((n, 256), 1) + half * 256
                s = jnp.where(seen, s, -BIG)
            scores.append(s)
            if not first:
                old.append((top[h, :, qs], total[h, :, qs], acc[h, :, qs]))
        new = []
        for n, (h, qcols, qs, half, lo, hi) in enumerate(chains):
            s = scores[n]
            best = jnp.max(s, axis=0, keepdims=True)
            if not first:
                best = jnp.maximum(old[n][0], best)
                alpha = jnp.exp2((old[n][0] - best) * FACTOR)
            e = jnp.exp2((s - best) * FACTOR)
            part = jnp.sum(e, axis=0, keepdims=True)
            values = jnp.concatenate(
                [values_of[t : t + 128] for t in range(lo, hi, 128)], axis=1
            )
            pv = jnp.dot(values, e.astype(BF16), preferred_element_type=F32)
            if not first:
                part = old[n][1] * alpha + part
                pv = old[n][2] * alpha + pv
            new.append((best, part, pv))
        for (best, part, pv), (h, qcols, qs, half, lo, hi) in zip(new, chains):
            if last:
                mine[qs, qcols] = (pv / part).T.astype(BF16)
            else:
                top[h, :, qs] = best
                total[h, :, qs] = part
                acc[h, :, qs] = pv

    def attend(d, g, first=False, last=False):
        def heads(r, carry):
            block_step(d, g, [r * HEADS_AT_ONCE + n for n in range(HEADS_AT_ONCE)], first, last)
            return carry

        lax.fori_loop(0, 4 // HEADS_AT_ONCE, heads, 0)

    out_cols = lambda g: pl.ds(pl.multiple_of(core * QCOLS + g * 512, 512), 512)

    def give(g):
        cols = slice(g * 512, g * 512 + 512)
        return copies.start(mine.at[other_rows, cols], out.at[:, out_cols(g)], partner)

    def arrive(step):
        for column, events in enumerate(ARRIVALS[step]):
            if events:

                @pl.when(cx == column)
                def _(events=events):
                    for n, d in events:
                        arrived(n, d)

    back = []
    for step, (d, g) in enumerate(ORDER):
        arrive(step)
        attend(d, g, first=d == 0, last=d == 2)
        if d == 2:
            back.append(give(g))
    for g in range(2):
        out[:, out_cols(g)] = mine[own_rows, g * 512 : g * 512 + 512]
    arrive(len(ORDER))
    for copy in back:
        copy.wait_recv()
    copies.drain()
    for n in range(PIECES):
        for cause in routes[n]:
            do("wait", n, cause)


def on_device(tokens, qkv_weight, route, offset, doc_lengths):
    half = HEAD_SIZE // 2
    freq = ROPE_BASE ** (-(jnp.arange(half, dtype=F32) * 2.0 / HEAD_SIZE))
    freq = jnp.concatenate([freq, freq])[None]
    vmem = pl.BlockSpec(memory_space=pltpu.VMEM)
    hbm = pl.BlockSpec(memory_space=pltpu.HBM)
    smem = pl.BlockSpec(memory_space=pltpu.SMEM)
    return pl.pallas_call(
        kernel,
        out_shape=jax.ShapeDtypeStruct((TOK, 2 * QCOLS), BF16),
        in_specs=[hbm, hbm, hbm, hbm, smem, vmem],
        out_specs=vmem,
        scratch_shapes=[
            pltpu.VMEM((TOK, MODEL), BF16),
            pltpu.VMEM((8, 2 * COLS), BF16),
            pltpu.VMEM((1, TOK), I32),
            pltpu.VMEM((1, TOK), I32),
            pltpu.VMEM((N_DP, SLOT, MODEL), BF16),
            pltpu.VMEM((N_DP, 8, 128), I32),
            pltpu.VMEM((N_DP, SLOT, MODEL), BF16),
            pltpu.VMEM((N_DP, 8, 128), I32),
            pltpu.VMEM((N_DP, SLOT, MODEL), BF16),
            pltpu.VMEM((8, COLS), F32),
            pltpu.VMEM((8, COLS), F32),
            pltpu.VMEM((N_DP, CHIPS, 16, COLS), BF16),
            pltpu.VMEM((CHIP_TOK, MODEL), BF16),
            pltpu.VMEM((CHIP_TOK, HEAD_SIZE), F32),
            pltpu.VMEM((CHIP_TOK, HEAD_SIZE), F32),
            pltpu.VMEM((CHIP_TOK, QCOLS), BF16),
            pltpu.VMEM((PIECES // 2, CHIP_TOK, HEAD_SIZE), BF16),
            pltpu.VMEM((PASSING, PIECES // 2, CHIP_TOK, HEAD_SIZE), BF16),
            pltpu.VMEM((CHIP_TOK, 128), BF16),
            pltpu.VMEM((REACH + 1, CHIP_TOK, 128), BF16),
            pltpu.VMEM((8, 1, CHIP_TOK), F32),
            pltpu.VMEM((8, 1, CHIP_TOK), F32),
            pltpu.VMEM((8, HEAD_SIZE, CHIP_TOK), F32),
            pltpu.VMEM((CHIP_TOK, QCOLS), BF16),
            pltpu.SemaphoreType.DMA((N_COPIES,)),
            pltpu.SemaphoreType.DMA((N_COPIES,)),
            pltpu.SemaphoreType.DMA((PIECES, LEGS)),
            pltpu.SemaphoreType.DMA((PIECES, PASSING)),
            pltpu.SemaphoreType.DMA((4,)),
        ],
        compiler_params=pltpu.CompilerParams(
            collective_id=0, has_side_effects=True, vmem_limit_bytes=50 * 2**20
        ),
    )(tokens, qkv_weight, route.reshape(1, TOK), offset.reshape(1, TOK), doc_lengths, freq)


def solution(mesh):
    in_specs = (
        P(("dp", "sp"), None),
        P(("dp", "sp"), None),
        P(("dp", "sp")),
        P(("dp", "sp")),
        P("dp", None),
    )
    out_specs = P(("dp", "sp"), None)
    return jax.shard_map(
        on_device, mesh=mesh, in_specs=in_specs, out_specs=out_specs, check_vma=False
    )
```

```python
import jax
import jax.numpy as jnp
from jax import lax
from jax.experimental import pallas as pl
from jax.experimental.pallas import tpu as pltpu
from jax.sharding import PartitionSpec as P

HEAD_SIZE = 128
ROPE_BASE = 500000.0
N_DP = 8
SIDE = 4
CHIPS = SIDE * SIDE
TOK = 256
CHIP_TOK = 2 * TOK
MODEL = 2048
SLOT = TOK // N_DP
QCOLS = 1024
KVCOLS = 256
COLS = QCOLS + 2 * KVCOLS
HALF = COLS // 2
REACH = 4
HEADS_AT_ONCE = 4
DOCS = 16
PIECES = 8
CROSSING = (2, 5, 7)
LEGS = 12
PASSING = 5
BIG = 2.0**100
FACTOR = HEAD_SIZE ** (-0.5) * 1.4426950408889634
EXTRA_RIGHT, EXTRA_LEFT = 4, 3
W_RIGHT, W_LEFT = 3, 4
PIECE_ORDER = (0, 3, 2, 1, 4, 6, 7, 5)
ORDER = ((0, 0), (4, 0), (0, 1), (1, 0), (4, 1), (3, 0), (1, 1), (2, 0), (3, 1), (2, 1))
ARRIVALS = (
    ((), (), (), ()),
    (((0, 4), (2, 5), (3, 4), (7, 5), (2, 4), (5, 5), (0, 1), (1, 4), (0, 3),), ((0, 1), (0, 4), (3, 1), (3, 4), (2, 1), (2, 4), (0, 3), (1, 1), (1, 4),), ((0, 1), (0, 4), (3, 1), (3, 4), (2, 1), (2, 4), (0, 3), (1, 1), (1, 4),), ((0, 3), (0, 1), (0, 4), (3, 3), (3, 1), (3, 4), (2, 3), (2, 1), (2, 4), (1, 3), (1, 1), (1, 4),)),
    (((3, 1), (4, 4), (3, 3),), ((3, 3), (4, 1), (4, 4),), ((3, 3), (4, 1), (4, 4),), ((4, 3), (4, 1), (4, 4),)),
    (((2, 1), (6, 4), (0, 2), (1, 1),), ((2, 3), (6, 1), (6, 4),), ((2, 2), (6, 1), (6, 4),), ((6, 3), (6, 1), (6, 4),)),
    (((7, 4), (1, 3), (4, 1), (5, 4), (3, 2),), ((0, 2), (7, 1), (7, 4), (1, 3), (5, 1), (5, 4),), ((2, 3), (7, 1), (7, 4), (1, 3), (5, 1), (5, 4),), ((7, 3), (7, 1), (7, 4), (5, 3), (5, 1), (5, 4),)),
    (((2, 3), (6, 1), (4, 3),), ((3, 2), (2, 2),), ((4, 3), (0, 2),), ((0, 2), (2, 2), (2, 5),)),
    (((7, 3), (6, 3), (7, 1), (5, 3), (1, 2), (5, 1),), ((4, 3),), ((6, 3), (3, 2),), ((3, 2), (7, 2), (7, 5),)),
    (((2, 2),), ((6, 3), (7, 3), (1, 2),), ((7, 2), (1, 2), (7, 3), (4, 2),), ((5, 2), (1, 2), (5, 5), (4, 2),)),
    (((4, 2), (7, 2),), ((7, 2), (5, 3),), ((5, 2), (6, 2), (5, 3),), ((6, 2),)),
    (((6, 2), (5, 2),), ((5, 2), (4, 2), (6, 2),), (), ()),
    ((), (), (), ()),
)
MESH = pl.DeviceIdType.MESH
F32 = jnp.float32
BF16 = jnp.bfloat16
I32 = jnp.int32


def iota(shape, dim):
    return lax.broadcasted_iota(I32, shape, dim)


class Copies:
    def __init__(self, send, recv):
        self.send, self.recv, self.made = send, recv, []

    def start(self, src, dst, device):
        n = len(self.made)
        copy = pltpu.make_async_remote_copy(
            src_ref=src,
            dst_ref=dst,
            send_sem=self.send.at[n],
            recv_sem=self.recv.at[n],
            device_id=device,
            device_id_type=MESH,
        )
        copy.start()
        self.made.append(copy)
        return copy

    def drain(self):
        for copy in self.made:
            copy.wait_send()


def greet(devices):
    barrier = pltpu.get_barrier_semaphore()
    for device in devices:
        pl.semaphore_signal(barrier, inc=1, device_id=device, device_id_type=MESH)
    return lambda: pl.semaphore_wait(barrier, len(devices))


N_COPIES = 1 + 7 + 7 + 2 * 7 + 2 * 2 * (4 + 16) + 4 + 2


def kernel(
    tokens_in, w_in, route_in, offset_in, lens, freq, out,
    tokens, w, route, offset,
    packed, ids, got, got_ids, extra, wsend, wrecv, wbuf, x,
    cosine, sine, q, kv, kvbuf, qdoc, kdoc, top, total, acc, mine,
    send, recv, leg_send, leg_recv, load,
):
    z = lax.axis_index("dp")
    sp = lax.axis_index("sp")
    core = lax.rem(sp, 2)
    chip = sp // 2
    cy, cx = chip // SIDE, lax.rem(chip, SIDE)
    partner = (z, sp + 1 - 2 * core)

    def at_z(d):
        return (lax.rem(z + d + N_DP, N_DP), sp)

    def place(dy, dx):
        return lax.rem(cy + dy + SIDE, SIDE) * SIDE + lax.rem(cx + dx + SIDE, SIDE)

    def at_chip(dy, dx):
        return (z, place(dy, dx) * 2 + core)

    def half_of(c):
        cols = lambda base, width: w[:, pl.ds(pl.multiple_of(base + c * width, 128), width)]
        return [
            (0, QCOLS, cols(0, QCOLS)),
            (QCOLS, KVCOLS, cols(2 * QCOLS, KVCOLS)),
            (QCOLS + KVCOLS, KVCOLS, cols(2 * QCOLS + 2 * KVCOLS, KVCOLS)),
        ]

    met = greet(
        [at_z(d) for d in range(1, N_DP)]
        + [partner]
        + [at_chip(0, 1), at_chip(0, -1), at_chip(1, 0), at_chip(-1, 0)]
    )
    loads = [
        pltpu.make_async_copy(here, there, load.at[n])
        for n, (here, there) in enumerate(
            [(w_in, w), (route_in, route), (offset_in, offset), (tokens_in, tokens)]
        )
    ]
    for copy in loads:
        copy.start()
    loads[0].wait()
    for base, width, part in half_of(1 - core):
        wsend[:, base : base + width] = part.astype(F32)

    met()
    copies = Copies(send, recv)

    swap = copies.start(wsend, wrecv, partner)

    for copy in loads[1:]:
        copy.wait()

    group = iota((8, TOK), 0)
    route_row = route[...]
    onehot = route_row == group
    before = (iota((TOK, TOK), 0) < iota((TOK, TOK), 1)).astype(F32).astype(BF16)
    rank = jnp.dot(
        onehot.astype(F32).astype(BF16), before, preferred_element_type=F32
    ).astype(I32)
    dest = jnp.where(rank < SLOT, group * SLOT + rank, N_DP * SLOT + rank - SLOT)
    dest = jnp.sum(jnp.where(onehot, dest, 0), axis=0, keepdims=True)

    def pack(block):
        pick = (iota((SLOT, TOK), 0) + block * SLOT == dest).astype(F32).astype(BF16)
        return jnp.dot(pick, tokens[...], preferred_element_type=F32).astype(BF16)

    def extra_ring(s):
        sent = []
        right, left = lax.rem(z - s + N_DP, N_DP), lax.rem(z + s, N_DP)
        if s < EXTRA_RIGHT:
            sent.append(copies.start(extra.at[right], extra.at[right], at_z(1)))
        if s < EXTRA_LEFT:
            sent.append(copies.start(extra.at[left], extra.at[left], at_z(-1)))
        return sent

    def w_ring(s):
        sent = []
        if s < W_RIGHT:
            here, there = (1 - s) % N_DP, -s % N_DP
            sent.append(copies.start(wbuf.at[here, chip], wbuf.at[there, chip], at_z(1)))
        if s < W_LEFT:
            sent.append(copies.start(wbuf.at[1 + s, chip], wbuf.at[2 + s, chip], at_z(-1)))
        return sent

    facts = jnp.where(
        group == 0,
        offset[...] - sp * TOK,
        jnp.where(group == 1, route_row, jnp.where(group == 2, 1, 0)),
    ).astype(F32).astype(BF16)
    lane = iota((TOK, TOK), 0) - z * SLOT
    lane_ok = jnp.where((lane >= 0) & (lane < SLOT), lane, -10 * TOK)

    def numbers_of(block):
        pick = (lane_ok + block * SLOT == dest).astype(F32).astype(BF16)
        found = lax.dot_general(
            facts, pick, (((1,), (1,)), ((), ())), preferred_element_type=F32
        ).astype(I32)
        number = found[1:2] * TOK + found[0:1] + found[2:3]
        return [number[:, 0:128], number[:, 128:256]]

    more = numbers_of(N_DP) + [jnp.zeros((4, 128), I32)]

    def prepare(d):
        to = lax.rem(z + d, N_DP)
        packed[to] = pack(to)
        ids[to] = jnp.concatenate(numbers_of(to) + more, axis=0)

    tokens_sent = []

    def send_tokens(d):
        to = lax.rem(z + d, N_DP)
        tokens_sent.append(copies.start(packed.at[to], got.at[z], at_z(d)))
        tokens_sent.append(copies.start(ids.at[to], got_ids.at[z], at_z(d)))

    for d in (1, 7):
        prepare(d)
        send_tokens(d)

    swap.wait_recv()
    for base, width, part in half_of(core):
        own = part.astype(F32)
        other = wrecv[:, base : base + width]
        first = jnp.where(core == 0, own, other)
        second = jnp.where(core == 0, other, own)
        wbuf[1, chip, :, base : base + width] = jnp.concatenate([first, second], axis=0).astype(BF16)
    w_tour = w_ring(0)

    extra[z] = pack(N_DP)
    tour = extra_ring(0)

    def w_step(s):
        for copy in w_tour:
            copy.wait_recv()
        return w_ring(s)

    def extra_step(s):
        for copy in tour:
            copy.wait_recv()
        return extra_ring(s)

    class Plane:
        def __init__(self, which, first, second, low, middle, high):
            self.which, self.first, self.second = which, first, second
            self.all, self.one, self.two = (low, high), (low, middle), (middle, high)

        def at(self, a, b):
            return (a * self.first[0] + b * self.second[0], a * self.first[1] + b * self.second[1])

        def send(self, a, b, blocks, to):
            ref = wbuf.at[
                pl.ds(blocks[0], blocks[1] - blocks[0]), place(*self.at(a, b)), :, pl.ds(self.which * HALF, HALF)
            ]
            return copies.start(ref, ref, at_chip(*self.at(*to)))

        def open(self):
            self.near = [self.send(0, 0, self.all, (1, 0)), self.send(0, 0, self.all, (-1, 0))]
            self.across = {}

        def spread(self, u):
            self.across[u] = [self.send(u, 0, self.all, (0, 1)), self.send(u, 0, self.all, (0, -1))]

        def forward(self):
            self.near[0].wait_recv()
            self.far = [self.send(-1, 0, self.one, (1, 0))]
            self.near[1].wait_recv()
            self.far.append(self.send(1, 0, self.two, (-1, 0)))

        def close(self):
            for copy in self.far:
                copy.wait_recv()

        def pass_on(self, u):
            self.across[u][0].wait_recv()
            one = self.send(u, -1, self.one, (0, 1))
            self.across[u][1].wait_recv()
            return [one, self.send(u, 1, self.two, (0, -1))]

    near, rest = (
        [Plane(0, (0, 1), (1, 0), *blocks), Plane(1, (1, 0), (0, 1), *blocks)]
        for blocks in ((0, 2, 3), (3, 5, 8))
    )
    last = []

    def open_plane(planes):
        for plane in planes:
            plane.open()
        for plane in planes:
            plane.spread(0)

    def widen(planes):
        for plane in planes:
            plane.forward()
        for plane in planes:
            plane.spread(-1)
            plane.spread(1)

    def finish(planes):
        for plane in planes:
            plane.close()
            plane.spread(2)

    def pass_on(planes, u):
        for plane in planes:
            last.extend(plane.pass_on(u))

    w_tour = w_step(1)
    open_plane(near)
    for d in (3, 2):
        prepare(d)
    tour = extra_step(1)
    widen(near)
    w_tour = w_step(2)
    tour = extra_step(2)
    send_tokens(3)
    for d in (5, 6, 4):
        prepare(d)
    finish(near)
    pass_on(near, 0)
    w_tour = w_step(3)
    send_tokens(5)
    send_tokens(2)
    pass_on(near, -1)
    tour = extra_step(3)
    send_tokens(6)
    send_tokens(4)
    pass_on(near, 1)
    w_tour = w_step(4)
    open_plane(rest)
    pass_on(near, 2)
    prepare(0)
    got[z] = packed[z]
    got_ids[z] = ids[z]

    lanes = iota((1, 128), 1)
    starts = jnp.full((1, 128), 2**30, I32)
    ends = jnp.full((1, 128), 2**30, I32)
    row = iota((CHIP_TOK, 128), 0) + chip * CHIP_TOK
    begin_of = jnp.zeros((CHIP_TOK, 128), I32)
    begin = lens[0, 0] * 0
    for e in range(DOCS):
        starts = jnp.where(lanes == e, begin, starts)
        begin_of = jnp.where(row >= begin, begin, begin_of)
        begin = begin + lens[0, e]
        ends = jnp.where(lanes == e, begin, ends)
    angle = (row - begin_of).astype(F32) * freq[...]
    cosine[...] = jnp.cos(angle)
    sine[...] = jnp.sin(angle) * jnp.where(lanes < 64, -1.0, 1.0)

    def member(base):
        point = iota((CHIP_TOK, 128), 0) + base
        return (point >= starts) & (point < ends)

    qdoc[...] = jnp.where(member(chip * CHIP_TOK), 1.0, 0.0).astype(BF16)
    for d in range(REACH + 1):
        kdoc[d] = jnp.where(member((chip - d) * CHIP_TOK), 0.0, -BIG).astype(BF16)

    widen(rest)
    finish(rest)
    pass_on(rest, 0)
    tour = extra_step(4)
    for u in (-1, 1, 2):
        pass_on(rest, u)

    for copy in tokens_sent:
        copy.wait_recv()
    mine_ids = iota((TOK, TOK), 0) + z * TOK + 1
    numbers = jnp.zeros((8, 128), I32)
    for source in range(N_DP):
        numbers += got_ids[source]
    to_place = [
        (jnp.concatenate([numbers[n : n + 1], numbers[n + 1 : n + 2]], axis=1) == mine_ids)
        .astype(F32)
        .astype(BF16)
        for n in (0, 2)
    ]
    own_rows = pl.ds(pl.multiple_of(core * TOK, TOK), TOK)
    other_rows = pl.ds(pl.multiple_of((1 - core) * TOK, TOK), TOK)
    shared = []
    for part in range(N_DP):
        from_z = lax.rem(z + part + N_DP - 1, N_DP)
        cols = pl.ds(pl.multiple_of(from_z * 256, 256), 256)
        rows = jnp.dot(
            to_place[0], got[:, :, cols].reshape(TOK, 256), preferred_element_type=F32
        ) + jnp.dot(
            to_place[1], extra[:, :, cols].reshape(TOK, 256), preferred_element_type=F32
        )
        x[own_rows, part * 256 : part * 256 + 256] = rows.astype(BF16)
        if part % 2:
            ready = x.at[own_rows, part * 256 - 256 : part * 256 + 256]
            shared.append(copies.start(ready, ready, partner))
    for copy in last:
        copy.wait_recv()

    def project(c, rows):
        cols = pl.ds(pl.multiple_of(c * 256, 256), 256)
        weights = wbuf[:, :, :, cols].reshape(MODEL, 256)
        return jnp.dot(x[rows], weights, preferred_element_type=F32).astype(BF16)

    def rotated(y, rows):
        parts = []
        for n in range(2):
            v = y[:, n * 128 : n * 128 + 128].astype(F32)
            parts.append((v * cosine[rows] + pltpu.roll(v, 64, 1) * sine[rows]).astype(BF16))
        return parts

    def project_keys(rows, base):
        keys = rotated(project(4, rows), rows)
        values = project(5, rows).astype(F32)
        for g in range(2):
            kv[2 * g, rows] = keys[g]
            for t in range(2):
                block = values[t * 128 : t * 128 + 128, g * 128 : g * 128 + 128]
                at = pl.ds(pl.multiple_of(base + t * 128, 128), 128)
                kv[2 * g + 1, at] = block.T.astype(BF16)

    def queries(rows):
        def query(c, carry):
            for n, part in enumerate(rotated(project(c, rows), rows)):
                q[rows, pl.ds(pl.multiple_of(c * 256 + n * 128, 128), 128)] = part
            return carry

        lax.fori_loop(0, 4, query, 0)

    project_keys(own_rows, core * TOK)
    queries(own_rows)
    for copy in shared:
        copy.wait_recv()
    project_keys(other_rows, (1 - core) * TOK)

    def piece(n):
        return n // 2, slice(n % 2 * 256, n % 2 * 256 + 256)

    def leg(n, number, d, to, source, when):
        copy = pltpu.make_async_remote_copy(
            src_ref=source,
            dst_ref=kvbuf.at[(d - 1, *piece(n))],
            send_sem=leg_send.at[n, number],
            recv_sem=leg_recv.at[n, d - 1],
            device_id=to,
            device_id_type=MESH,
        )
        return copy, when

    def legs(n):
        own, came = kv.at[piece(n)], lambda d: kvbuf.at[(d - 1, *piece(n))]
        right, left, down = at_chip(0, 1), at_chip(0, -1), at_chip(1, 0)
        inner = (cx == 1) | (cx == 2)
        first = [(4, down, own, None), (1, right, own, cx < 3), (3, left, own, cx == 0)]
        if n not in CROSSING:
            return {
                0: first,
                4: [(3, left, came(4), cx > 0), (1, right, came(4), cx == 3)],
                1: [(2, right, came(1), inner)],
                3: [(2, left, came(3), inner)],
            }
        return {
            0: first + [(PASSING, left, own, cx == 1)],
            4: [(3, left, came(4), cx > 1), (1, right, came(4), cx == 3)],
            1: [(2, right, came(1), cx == 0), (PASSING, down, came(1), cx == 3)],
            PASSING: [
                (2, left, came(PASSING), cx == 0),
                (3, down, came(PASSING), cx == 0),
                (2, right, came(PASSING), cx == 3),
            ],
            3: [(2, left, came(3), cx == 3)],
        }

    routes, number = [], 0
    for n in range(PIECES):
        number = 0
        route_of = {}
        for cause, parts in legs(n).items():
            route_of[cause] = []
            for d, to, source, when in parts:
                route_of[cause].append(leg(n, number, d, to, source, when))
                number += 1
        routes.append(route_of)

    def do(action, n, cause):
        for copy, when in routes[n].get(cause, []):
            run = copy.start if action == "start" else copy.wait_send
            if when is None:
                run()
            else:
                pl.when(when)(run)

    def arrived(n, d):
        wait = pltpu.make_async_remote_copy(
            src_ref=kvbuf.at[(d - 1, *piece(n))],
            dst_ref=kvbuf.at[(d - 1, *piece(n))],
            send_sem=leg_send.at[n, 0],
            recv_sem=leg_recv.at[n, d - 1],
            device_id=partner,
            device_id_type=MESH,
        ).wait_recv
        wait()
        do("start", n, d)

    for n in PIECE_ORDER:
        do("start", n, 0)

    queries(other_rows)

    def block_step(d, g, heads, first, last):
        keys_of = kv.at[2 * g] if d == 0 else kvbuf.at[d - 1, 2 * g]
        values_of = kv.at[2 * g + 1] if d == 0 else kvbuf.at[d - 1, 2 * g + 1]
        chains = []
        for r in heads:
            h = g * 4 + r
            qcols = pl.ds(pl.multiple_of(h * 128, 128), 128)
            for half in range(2):
                lo, hi = 0, 512
                if d == 0 and half == 0:
                    hi = 256
                if d == REACH and half == 1:
                    lo = 256
                chains.append((h, qcols, slice(half * 256, half * 256 + 256), half, lo, hi))
        scores, old = [], []
        for h, qcols, qs, half, lo, hi in chains:
            keys = jnp.concatenate([keys_of[lo:hi], kdoc[d, lo:hi]], axis=1)
            query = jnp.concatenate([q[qs, qcols], qdoc[qs]], axis=1)
            s = lax.dot_general(
                keys, query, (((1,), (1,)), ((), ())), preferred_element_type=F32
            )
            if d == 0:
                n = hi - lo
                seen = iota((n, 256), 0) + lo <= iota((n, 256), 1) + half * 256
                s = jnp.where(seen, s, -BIG)
            scores.append(s)
            if not first:
                old.append((top[h, :, qs], total[h, :, qs], acc[h, :, qs]))
        new = []
        for n, (h, qcols, qs, half, lo, hi) in enumerate(chains):
            s = scores[n]
            best = jnp.max(s, axis=0, keepdims=True)
            if not first:
                best = jnp.maximum(old[n][0], best)
                alpha = jnp.exp2((old[n][0] - best) * FACTOR)
            e = jnp.exp2((s - best) * FACTOR)
            part = jnp.sum(e, axis=0, keepdims=True)
            values = jnp.concatenate(
                [values_of[t : t + 128] for t in range(lo, hi, 128)], axis=1
            )
            pv = jnp.dot(values, e.astype(BF16), preferred_element_type=F32)
            if not first:
                part = old[n][1] * alpha + part
                pv = old[n][2] * alpha + pv
            new.append((best, part, pv))
        for (best, part, pv), (h, qcols, qs, half, lo, hi) in zip(new, chains):
            if last:
                mine[qs, qcols] = (pv / part).T.astype(BF16)
            else:
                top[h, :, qs] = best
                total[h, :, qs] = part
                acc[h, :, qs] = pv

    def attend(d, g, first=False, last=False):
        def heads(r, carry):
            block_step(d, g, [r * HEADS_AT_ONCE + n for n in range(HEADS_AT_ONCE)], first, last)
            return carry

        lax.fori_loop(0, 4 // HEADS_AT_ONCE, heads, 0)

    out_cols = lambda g: pl.ds(pl.multiple_of(core * QCOLS + g * 512, 512), 512)

    def give(g):
        cols = slice(g * 512, g * 512 + 512)
        return copies.start(mine.at[other_rows, cols], out.at[:, out_cols(g)], partner)

    def arrive(step):
        for column, events in enumerate(ARRIVALS[step]):
            if events:

                @pl.when(cx == column)
                def _(events=events):
                    for n, d in events:
                        arrived(n, d)

    back = []
    for step, (d, g) in enumerate(ORDER):
        arrive(step)
        attend(d, g, first=d == 0, last=d == 2)
        if d == 2:
            back.append(give(g))
    for g in range(2):
        out[:, out_cols(g)] = mine[own_rows, g * 512 : g * 512 + 512]
    arrive(len(ORDER))
    for copy in back:
        copy.wait_recv()
    copies.drain()
    for n in range(PIECES):
        for cause in routes[n]:
            do("wait", n, cause)


def on_device(tokens, qkv_weight, route, offset, doc_lengths):
    half = HEAD_SIZE // 2
    freq = ROPE_BASE ** (-(jnp.arange(half, dtype=F32) * 2.0 / HEAD_SIZE))
    freq = jnp.concatenate([freq, freq])[None]
    vmem = pl.BlockSpec(memory_space=pltpu.VMEM)
    hbm = pl.BlockSpec(memory_space=pltpu.HBM)
    smem = pl.BlockSpec(memory_space=pltpu.SMEM)
    return pl.pallas_call(
        kernel,
        out_shape=jax.ShapeDtypeStruct((TOK, 2 * QCOLS), BF16),
        in_specs=[hbm, hbm, hbm, hbm, smem, vmem],
        out_specs=vmem,
        scratch_shapes=[
            pltpu.VMEM((TOK, MODEL), BF16),
            pltpu.VMEM((8, 2 * COLS), BF16),
            pltpu.VMEM((1, TOK), I32),
            pltpu.VMEM((1, TOK), I32),
            pltpu.VMEM((N_DP, SLOT, MODEL), BF16),
            pltpu.VMEM((N_DP, 8, 128), I32),
            pltpu.VMEM((N_DP, SLOT, MODEL), BF16),
            pltpu.VMEM((N_DP, 8, 128), I32),
            pltpu.VMEM((N_DP, SLOT, MODEL), BF16),
            pltpu.VMEM((8, COLS), F32),
            pltpu.VMEM((8, COLS), F32),
            pltpu.VMEM((N_DP, CHIPS, 16, COLS), BF16),
            pltpu.VMEM((CHIP_TOK, MODEL), BF16),
            pltpu.VMEM((CHIP_TOK, HEAD_SIZE), F32),
            pltpu.VMEM((CHIP_TOK, HEAD_SIZE), F32),
            pltpu.VMEM((CHIP_TOK, QCOLS), BF16),
            pltpu.VMEM((PIECES // 2, CHIP_TOK, HEAD_SIZE), BF16),
            pltpu.VMEM((PASSING, PIECES // 2, CHIP_TOK, HEAD_SIZE), BF16),
            pltpu.VMEM((CHIP_TOK, 128), BF16),
            pltpu.VMEM((REACH + 1, CHIP_TOK, 128), BF16),
            pltpu.VMEM((8, 1, CHIP_TOK), F32),
            pltpu.VMEM((8, 1, CHIP_TOK), F32),
            pltpu.VMEM((8, HEAD_SIZE, CHIP_TOK), F32),
            pltpu.VMEM((CHIP_TOK, QCOLS), BF16),
            pltpu.SemaphoreType.DMA((N_COPIES,)),
            pltpu.SemaphoreType.DMA((N_COPIES,)),
            pltpu.SemaphoreType.DMA((PIECES, LEGS)),
            pltpu.SemaphoreType.DMA((PIECES, PASSING)),
            pltpu.SemaphoreType.DMA((4,)),
        ],
        compiler_params=pltpu.CompilerParams(
            collective_id=0, has_side_effects=True, vmem_limit_bytes=50 * 2**20
        ),
    )(tokens, qkv_weight, route.reshape(1, TOK), offset.reshape(1, TOK), doc_lengths, freq)


def solution(mesh):
    in_specs = (
        P(("dp", "sp"), None),
        P(("dp", "sp"), None),
        P(("dp", "sp")),
        P(("dp", "sp")),
        P("dp", None),
    )
    out_specs = P(("dp", "sp"), None)
    return jax.shard_map(
        on_device, mesh=mesh, in_specs=in_specs, out_specs=out_specs, check_vma=False
    )
```

```python
import jax
import jax.numpy as jnp
from jax import lax
from jax.experimental import pallas as pl
from jax.experimental.pallas import tpu as pltpu
from jax.sharding import PartitionSpec as P

HEAD_SIZE = 128
ROPE_BASE = 500000.0
N_DP = 8
SIDE = 4
CHIPS = SIDE * SIDE
TOK = 256
CHIP_TOK = 2 * TOK
MODEL = 2048
SLOT = TOK // N_DP
QCOLS = 1024
KVCOLS = 256
COLS = QCOLS + 2 * KVCOLS
HALF = COLS // 2
REACH = 4
HEADS_AT_ONCE = 4
DOCS = 16
PIECES = 8
CROSSING = (1, 3, 5)
LEGS = 12
PASSING = 5
BIG = 2.0**100
FACTOR = HEAD_SIZE ** (-0.5) * 1.4426950408889634
EXTRA_RIGHT, EXTRA_LEFT = 4, 3
W_RIGHT, W_LEFT = 3, 4
PIECE_ORDER = (0, 2, 4, 6, 1, 3, 7, 5)
ORDER = ((0, 1), (0, 0), (4, 0), (4, 1), (1, 0), (3, 0), (1, 1), (2, 0), (3, 1), (2, 1))
ARRIVALS = (
    (((0, 4), (2, 4),), ((0, 1), (0, 4), (2, 1), (2, 4),), ((0, 1), (0, 4), (2, 1), (2, 4),), ((0, 3), (0, 1), (0, 4), (2, 3), (2, 1), (2, 4),)),
    (((4, 4), (1, 5),), ((4, 1), (4, 4),), ((4, 1), (4, 4),), ((4, 3), (4, 1), (4, 4),)),
    (((0, 1), (6, 4), (3, 5), (1, 4), (2, 1), (5, 5), (3, 4), (0, 3),), ((0, 3), (6, 1), (6, 4), (2, 3), (1, 1), (1, 4), (4, 3), (3, 1), (3, 4),), ((0, 3), (6, 1), (6, 4), (1, 1), (1, 4), (2, 3), (3, 1), (3, 4),), ((6, 3), (6, 1), (6, 4), (1, 3), (1, 1), (1, 4), (3, 3), (3, 1), (3, 4),)),
    (((4, 1), (7, 4), (2, 3), (6, 1), (5, 4), (4, 3),), ((0, 2), (7, 1), (7, 4), (6, 3), (5, 1), (5, 4),), ((4, 3), (7, 1), (7, 4), (6, 3), (5, 1), (5, 4),), ((7, 3), (7, 1), (7, 4), (5, 3), (5, 1), (5, 4),)),
    (((1, 1), (1, 3), (0, 2), (3, 1),), ((1, 3),), ((1, 2), (0, 2),), ((0, 2), (1, 2), (1, 5),)),
    (((3, 3), (6, 3), (7, 1),), ((2, 2), (3, 3),), ((1, 3), (2, 2), (3, 2), (4, 2), (3, 3),), ((2, 2), (3, 2), (3, 5),)),
    (((5, 3), (2, 2), (5, 1), (4, 2), (1, 2),), ((1, 2), (4, 2),), ((6, 2), (7, 3),), ((4, 2), (5, 2), (5, 5), (6, 2),)),
    (((7, 3), (3, 2),), ((3, 2), (7, 3),), ((7, 2), (5, 2),), ((7, 2),)),
    (((6, 2), (5, 2),), ((6, 2), (5, 2), (5, 3),), ((5, 3),), ()),
    (((7, 2),), ((7, 2),), (), ()),
    ((), (), (), ()),
)
MESH = pl.DeviceIdType.MESH
F32 = jnp.float32
BF16 = jnp.bfloat16
I32 = jnp.int32


def iota(shape, dim):
    return lax.broadcasted_iota(I32, shape, dim)


class Copies:
    def __init__(self, send, recv):
        self.send, self.recv, self.made = send, recv, []

    def start(self, src, dst, device):
        n = len(self.made)
        copy = pltpu.make_async_remote_copy(
            src_ref=src,
            dst_ref=dst,
            send_sem=self.send.at[n],
            recv_sem=self.recv.at[n],
            device_id=device,
            device_id_type=MESH,
        )
        copy.start()
        self.made.append(copy)
        return copy

    def drain(self):
        for copy in self.made:
            copy.wait_send()


def greet(devices):
    barrier = pltpu.get_barrier_semaphore()
    for device in devices:
        pl.semaphore_signal(barrier, inc=1, device_id=device, device_id_type=MESH)
    return lambda: pl.semaphore_wait(barrier, len(devices))


N_COPIES = 1 + 7 + 7 + 2 * 7 + 2 * 2 * (4 + 16) + 4 + 2


def kernel(
    tokens_in, w_in, route_in, offset_in, lens, freq, out,
    tokens, w, route, offset,
    packed, ids, got, got_ids, extra, wsend, wrecv, wbuf, x,
    cosine, sine, q, kv, kvbuf, qdoc, kdoc, top, total, acc, mine,
    send, recv, leg_send, leg_recv, load,
):
    z = lax.axis_index("dp")
    sp = lax.axis_index("sp")
    core = lax.rem(sp, 2)
    chip = sp // 2
    cy, cx = chip // SIDE, lax.rem(chip, SIDE)
    partner = (z, sp + 1 - 2 * core)

    def at_z(d):
        return (lax.rem(z + d + N_DP, N_DP), sp)

    def place(dy, dx):
        return lax.rem(cy + dy + SIDE, SIDE) * SIDE + lax.rem(cx + dx + SIDE, SIDE)

    def at_chip(dy, dx):
        return (z, place(dy, dx) * 2 + core)

    def half_of(c):
        cols = lambda base, width: w[:, pl.ds(pl.multiple_of(base + c * width, 128), width)]
        return [
            (0, QCOLS, cols(0, QCOLS)),
            (QCOLS, KVCOLS, cols(2 * QCOLS, KVCOLS)),
            (QCOLS + KVCOLS, KVCOLS, cols(2 * QCOLS + 2 * KVCOLS, KVCOLS)),
        ]

    met = greet(
        [at_z(d) for d in range(1, N_DP)]
        + [partner]
        + [at_chip(0, 1), at_chip(0, -1), at_chip(1, 0), at_chip(-1, 0)]
    )
    loads = [
        pltpu.make_async_copy(here, there, load.at[n])
        for n, (here, there) in enumerate(
            [(w_in, w), (route_in, route), (offset_in, offset), (tokens_in, tokens)]
        )
    ]
    for copy in loads:
        copy.start()
    loads[0].wait()
    for base, width, part in half_of(1 - core):
        wsend[:, base : base + width] = part.astype(F32)

    met()
    copies = Copies(send, recv)

    swap = copies.start(wsend, wrecv, partner)

    for copy in loads[1:]:
        copy.wait()

    group = iota((8, TOK), 0)
    route_row = route[...]
    onehot = route_row == group
    before = (iota((TOK, TOK), 0) < iota((TOK, TOK), 1)).astype(F32).astype(BF16)
    rank = jnp.dot(
        onehot.astype(F32).astype(BF16), before, preferred_element_type=F32
    ).astype(I32)
    dest = jnp.where(rank < SLOT, group * SLOT + rank, N_DP * SLOT + rank - SLOT)
    dest = jnp.sum(jnp.where(onehot, dest, 0), axis=0, keepdims=True)

    def pack(block):
        pick = (iota((SLOT, TOK), 0) + block * SLOT == dest).astype(F32).astype(BF16)
        return jnp.dot(pick, tokens[...], preferred_element_type=F32).astype(BF16)

    def extra_ring(s):
        sent = []
        right, left = lax.rem(z - s + N_DP, N_DP), lax.rem(z + s, N_DP)
        if s < EXTRA_RIGHT:
            sent.append(copies.start(extra.at[right], extra.at[right], at_z(1)))
        if s < EXTRA_LEFT:
            sent.append(copies.start(extra.at[left], extra.at[left], at_z(-1)))
        return sent

    def w_ring(s):
        sent = []
        if s < W_RIGHT:
            here, there = (1 - s) % N_DP, -s % N_DP
            sent.append(copies.start(wbuf.at[here, chip], wbuf.at[there, chip], at_z(1)))
        if s < W_LEFT:
            sent.append(copies.start(wbuf.at[1 + s, chip], wbuf.at[2 + s, chip], at_z(-1)))
        return sent

    facts = jnp.where(
        group == 0,
        offset[...] - sp * TOK,
        jnp.where(group == 1, route_row, jnp.where(group == 2, 1, 0)),
    ).astype(F32).astype(BF16)
    lane = iota((TOK, TOK), 0) - z * SLOT
    lane_ok = jnp.where((lane >= 0) & (lane < SLOT), lane, -10 * TOK)

    def numbers_of(block):
        pick = (lane_ok + block * SLOT == dest).astype(F32).astype(BF16)
        found = lax.dot_general(
            facts, pick, (((1,), (1,)), ((), ())), preferred_element_type=F32
        ).astype(I32)
        number = found[1:2] * TOK + found[0:1] + found[2:3]
        return [number[:, 0:128], number[:, 128:256]]

    more = numbers_of(N_DP) + [jnp.zeros((4, 128), I32)]

    def prepare(d):
        to = lax.rem(z + d, N_DP)
        packed[to] = pack(to)
        ids[to] = jnp.concatenate(numbers_of(to) + more, axis=0)

    tokens_sent = []

    def send_tokens(d):
        to = lax.rem(z + d, N_DP)
        tokens_sent.append(copies.start(packed.at[to], got.at[z], at_z(d)))
        tokens_sent.append(copies.start(ids.at[to], got_ids.at[z], at_z(d)))

    for d in (1, 7):
        prepare(d)
        send_tokens(d)

    swap.wait_recv()
    for base, width, part in half_of(core):
        own = part.astype(F32)
        other = wrecv[:, base : base + width]
        first = jnp.where(core == 0, own, other)
        second = jnp.where(core == 0, other, own)
        wbuf[1, chip, :, base : base + width] = jnp.concatenate([first, second], axis=0).astype(BF16)
    w_tour = w_ring(0)

    extra[z] = pack(N_DP)
    tour = extra_ring(0)

    def w_step(s):
        for copy in w_tour:
            copy.wait_recv()
        return w_ring(s)

    def extra_step(s):
        for copy in tour:
            copy.wait_recv()
        return extra_ring(s)

    class Plane:
        def __init__(self, which, first, second, low, middle, high):
            self.which, self.first, self.second = which, first, second
            self.all, self.one, self.two = (low, high), (low, middle), (middle, high)

        def at(self, a, b):
            return (a * self.first[0] + b * self.second[0], a * self.first[1] + b * self.second[1])

        def send(self, a, b, blocks, to):
            ref = wbuf.at[
                pl.ds(blocks[0], blocks[1] - blocks[0]), place(*self.at(a, b)), :, pl.ds(self.which * HALF, HALF)
            ]
            return copies.start(ref, ref, at_chip(*self.at(*to)))

        def open(self):
            self.near = [self.send(0, 0, self.all, (1, 0)), self.send(0, 0, self.all, (-1, 0))]
            self.across = {}

        def spread(self, u):
            self.across[u] = [self.send(u, 0, self.all, (0, 1)), self.send(u, 0, self.all, (0, -1))]

        def forward(self):
            self.near[0].wait_recv()
            self.far = [self.send(-1, 0, self.one, (1, 0))]
            self.near[1].wait_recv()
            self.far.append(self.send(1, 0, self.two, (-1, 0)))

        def close(self):
            for copy in self.far:
                copy.wait_recv()

        def pass_on(self, u):
            self.across[u][0].wait_recv()
            one = self.send(u, -1, self.one, (0, 1))
            self.across[u][1].wait_recv()
            return [one, self.send(u, 1, self.two, (0, -1))]

    near, rest = (
        [Plane(0, (0, 1), (1, 0), *blocks), Plane(1, (1, 0), (0, 1), *blocks)]
        for blocks in ((0, 2, 3), (3, 5, 8))
    )
    last = []

    def open_plane(planes):
        for plane in planes:
            plane.open()
        for plane in planes:
            plane.spread(0)

    def widen(planes):
        for plane in planes:
            plane.forward()
        for plane in planes:
            plane.spread(-1)
            plane.spread(1)

    def finish(planes):
        for plane in planes:
            plane.close()
            plane.spread(2)

    def pass_on(planes, u):
        for plane in planes:
            last.extend(plane.pass_on(u))

    w_tour = w_step(1)
    open_plane(near)
    for d in (3, 2):
        prepare(d)
    tour = extra_step(1)
    widen(near)
    w_tour = w_step(2)
    tour = extra_step(2)
    send_tokens(3)
    for d in (5, 6, 4):
        prepare(d)
    finish(near)
    pass_on(near, 0)
    w_tour = w_step(3)
    send_tokens(5)
    send_tokens(2)
    pass_on(near, -1)
    tour = extra_step(3)
    send_tokens(6)
    send_tokens(4)
    pass_on(near, 1)
    w_tour = w_step(4)
    open_plane(rest)
    pass_on(near, 2)
    prepare(0)
    got[z] = packed[z]
    got_ids[z] = ids[z]

    lanes = iota((1, 128), 1)
    starts = jnp.full((1, 128), 2**30, I32)
    ends = jnp.full((1, 128), 2**30, I32)
    row = iota((CHIP_TOK, 128), 0) + chip * CHIP_TOK
    begin_of = jnp.zeros((CHIP_TOK, 128), I32)
    begin = lens[0, 0] * 0
    for e in range(DOCS):
        starts = jnp.where(lanes == e, begin, starts)
        begin_of = jnp.where(row >= begin, begin, begin_of)
        begin = begin + lens[0, e]
        ends = jnp.where(lanes == e, begin, ends)
    angle = (row - begin_of).astype(F32) * freq[...]
    cosine[...] = jnp.cos(angle)
    sine[...] = jnp.sin(angle) * jnp.where(lanes < 64, -1.0, 1.0)

    def member(base):
        point = iota((CHIP_TOK, 128), 0) + base
        return (point >= starts) & (point < ends)

    qdoc[...] = jnp.where(member(chip * CHIP_TOK), 1.0, 0.0).astype(BF16)
    for d in range(REACH + 1):
        kdoc[d] = jnp.where(member((chip - d) * CHIP_TOK), 0.0, -BIG).astype(BF16)

    widen(rest)
    finish(rest)
    pass_on(rest, 0)
    tour = extra_step(4)
    for u in (-1, 1, 2):
        pass_on(rest, u)

    for copy in tokens_sent:
        copy.wait_recv()
    mine_ids = iota((TOK, TOK), 0) + z * TOK + 1
    numbers = jnp.zeros((8, 128), I32)
    for source in range(N_DP):
        numbers += got_ids[source]
    to_place = [
        (jnp.concatenate([numbers[n : n + 1], numbers[n + 1 : n + 2]], axis=1) == mine_ids)
        .astype(F32)
        .astype(BF16)
        for n in (0, 2)
    ]
    own_rows = pl.ds(pl.multiple_of(core * TOK, TOK), TOK)
    other_rows = pl.ds(pl.multiple_of((1 - core) * TOK, TOK), TOK)
    shared = []
    for part in range(N_DP):
        from_z = lax.rem(z + part + N_DP - 1, N_DP)
        cols = pl.ds(pl.multiple_of(from_z * 256, 256), 256)
        rows = jnp.dot(
            to_place[0], got[:, :, cols].reshape(TOK, 256), preferred_element_type=F32
        ) + jnp.dot(
            to_place[1], extra[:, :, cols].reshape(TOK, 256), preferred_element_type=F32
        )
        x[own_rows, part * 256 : part * 256 + 256] = rows.astype(BF16)
        if part % 2:
            ready = x.at[own_rows, part * 256 - 256 : part * 256 + 256]
            shared.append(copies.start(ready, ready, partner))
    for copy in last:
        copy.wait_recv()

    def project(c, rows):
        cols = pl.ds(pl.multiple_of(c * 256, 256), 256)
        weights = wbuf[:, :, :, cols].reshape(MODEL, 256)
        return jnp.dot(x[rows], weights, preferred_element_type=F32).astype(BF16)

    def rotated(y, rows):
        parts = []
        for n in range(2):
            v = y[:, n * 128 : n * 128 + 128].astype(F32)
            parts.append((v * cosine[rows] + pltpu.roll(v, 64, 1) * sine[rows]).astype(BF16))
        return parts

    def project_keys(rows, base):
        keys = rotated(project(4, rows), rows)
        values = project(5, rows).astype(F32)
        for g in range(2):
            kv[2 * g, rows] = keys[g]
            for t in range(2):
                block = values[t * 128 : t * 128 + 128, g * 128 : g * 128 + 128]
                at = pl.ds(pl.multiple_of(base + t * 128, 128), 128)
                kv[2 * g + 1, at] = block.T.astype(BF16)

    def queries(rows):
        def query(c, carry):
            for n, part in enumerate(rotated(project(c, rows), rows)):
                q[rows, pl.ds(pl.multiple_of(c * 256 + n * 128, 128), 128)] = part
            return carry

        lax.fori_loop(0, 4, query, 0)

    def piece(n):
        return n // 2, (own_rows, other_rows)[n % 2]

    def leg(n, number, d, to, source, when):
        copy = pltpu.make_async_remote_copy(
            src_ref=source,
            dst_ref=kvbuf.at[(d - 1, *piece(n))],
            send_sem=leg_send.at[n, number],
            recv_sem=leg_recv.at[n, d - 1],
            device_id=to,
            device_id_type=MESH,
        )
        return copy, when

    def legs(n):
        own, came = kv.at[piece(n)], lambda d: kvbuf.at[(d - 1, *piece(n))]
        right, left, down = at_chip(0, 1), at_chip(0, -1), at_chip(1, 0)
        inner = (cx == 1) | (cx == 2)
        first = [(4, down, own, None), (1, right, own, cx < 3), (3, left, own, cx == 0)]
        if n not in CROSSING:
            return {
                0: first,
                4: [(3, left, came(4), cx > 0), (1, right, came(4), cx == 3)],
                1: [(2, right, came(1), inner)],
                3: [(2, left, came(3), inner)],
            }
        return {
            0: first + [(PASSING, left, own, cx == 1)],
            4: [(3, left, came(4), cx > 1), (1, right, came(4), cx == 3)],
            1: [(2, right, came(1), cx == 0), (PASSING, down, came(1), cx == 3)],
            PASSING: [
                (2, left, came(PASSING), cx == 0),
                (3, down, came(PASSING), cx == 0),
                (2, right, came(PASSING), cx == 3),
            ],
            3: [(2, left, came(3), cx == 3)],
        }

    routes, number = [], 0
    for n in range(PIECES):
        number = 0
        route_of = {}
        for cause, parts in legs(n).items():
            route_of[cause] = []
            for d, to, source, when in parts:
                route_of[cause].append(leg(n, number, d, to, source, when))
                number += 1
        routes.append(route_of)

    def do(action, n, cause):
        for copy, when in routes[n].get(cause, []):
            run = copy.start if action == "start" else copy.wait_send
            if when is None:
                run()
            else:
                pl.when(when)(run)

    def arrived(n, d):
        wait = pltpu.make_async_remote_copy(
            src_ref=kvbuf.at[(d - 1, *piece(n))],
            dst_ref=kvbuf.at[(d - 1, *piece(n))],
            send_sem=leg_send.at[n, 0],
            recv_sem=leg_recv.at[n, d - 1],
            device_id=partner,
            device_id_type=MESH,
        ).wait_recv
        wait()
        do("start", n, d)

    project_keys(own_rows, core * TOK)
    for n in PIECE_ORDER[:4]:
        do("start", n, 0)
    queries(own_rows)
    for copy in shared:
        copy.wait_recv()
    project_keys(other_rows, (1 - core) * TOK)

    for n in PIECE_ORDER[4:]:
        do("start", n, 0)
    queries(other_rows)

    def block_step(d, g, heads, first, last):
        keys_of = kv.at[2 * g] if d == 0 else kvbuf.at[d - 1, 2 * g]
        values_of = kv.at[2 * g + 1] if d == 0 else kvbuf.at[d - 1, 2 * g + 1]
        chains = []
        for r in heads:
            h = g * 4 + r
            qcols = pl.ds(pl.multiple_of(h * 128, 128), 128)
            for half in range(2):
                lo, hi = 0, 512
                if d == 0 and half == 0:
                    hi = 256
                if d == REACH and half == 1:
                    lo = 256
                chains.append((h, qcols, slice(half * 256, half * 256 + 256), half, lo, hi))
        scores, old = [], []
        for h, qcols, qs, half, lo, hi in chains:
            keys = jnp.concatenate([keys_of[lo:hi], kdoc[d, lo:hi]], axis=1)
            query = jnp.concatenate([q[qs, qcols], qdoc[qs]], axis=1)
            s = lax.dot_general(
                keys, query, (((1,), (1,)), ((), ())), preferred_element_type=F32
            )
            if d == 0:
                n = hi - lo
                seen = iota((n, 256), 0) + lo <= iota((n, 256), 1) + half * 256
                s = jnp.where(seen, s, -BIG)
            scores.append(s)
            if not first:
                old.append((top[h, :, qs], total[h, :, qs], acc[h, :, qs]))
        new = []
        for n, (h, qcols, qs, half, lo, hi) in enumerate(chains):
            s = scores[n]
            best = jnp.max(s, axis=0, keepdims=True)
            if not first:
                best = jnp.maximum(old[n][0], best)
                alpha = jnp.exp2((old[n][0] - best) * FACTOR)
            e = jnp.exp2((s - best) * FACTOR)
            part = jnp.sum(e, axis=0, keepdims=True)
            values = jnp.concatenate(
                [values_of[t : t + 128] for t in range(lo, hi, 128)], axis=1
            )
            pv = jnp.dot(values, e.astype(BF16), preferred_element_type=F32)
            if not first:
                part = old[n][1] * alpha + part
                pv = old[n][2] * alpha + pv
            new.append((best, part, pv))
        for (best, part, pv), (h, qcols, qs, half, lo, hi) in zip(new, chains):
            if last:
                mine[qs, qcols] = (pv / part).T.astype(BF16)
            else:
                top[h, :, qs] = best
                total[h, :, qs] = part
                acc[h, :, qs] = pv

    def attend(d, g, first=False, last=False):
        def heads(r, carry):
            block_step(d, g, [r * HEADS_AT_ONCE + n for n in range(HEADS_AT_ONCE)], first, last)
            return carry

        lax.fori_loop(0, 4 // HEADS_AT_ONCE, heads, 0)

    out_cols = lambda g: pl.ds(pl.multiple_of(core * QCOLS + g * 512, 512), 512)

    def give(g):
        cols = slice(g * 512, g * 512 + 512)
        return copies.start(mine.at[other_rows, cols], out.at[:, out_cols(g)], partner)

    def arrive(step):
        for column, events in enumerate(ARRIVALS[step]):
            if events:

                @pl.when(cx == column)
                def _(events=events):
                    for n, d in events:
                        arrived(n, d)

    back = []
    for step, (d, g) in enumerate(ORDER):
        arrive(step)
        attend(d, g, first=d == 0, last=d == 2)
        if d == 2:
            back.append(give(g))
    for g in range(2):
        out[:, out_cols(g)] = mine[own_rows, g * 512 : g * 512 + 512]
    arrive(len(ORDER))
    for copy in back:
        copy.wait_recv()
    copies.drain()
    for n in range(PIECES):
        for cause in routes[n]:
            do("wait", n, cause)


def on_device(tokens, qkv_weight, route, offset, doc_lengths):
    half = HEAD_SIZE // 2
    freq = ROPE_BASE ** (-(jnp.arange(half, dtype=F32) * 2.0 / HEAD_SIZE))
    freq = jnp.concatenate([freq, freq])[None]
    vmem = pl.BlockSpec(memory_space=pltpu.VMEM)
    hbm = pl.BlockSpec(memory_space=pltpu.HBM)
    smem = pl.BlockSpec(memory_space=pltpu.SMEM)
    return pl.pallas_call(
        kernel,
        out_shape=jax.ShapeDtypeStruct((TOK, 2 * QCOLS), BF16),
        in_specs=[hbm, hbm, hbm, hbm, smem, vmem],
        out_specs=vmem,
        scratch_shapes=[
            pltpu.VMEM((TOK, MODEL), BF16),
            pltpu.VMEM((8, 2 * COLS), BF16),
            pltpu.VMEM((1, TOK), I32),
            pltpu.VMEM((1, TOK), I32),
            pltpu.VMEM((N_DP, SLOT, MODEL), BF16),
            pltpu.VMEM((N_DP, 8, 128), I32),
            pltpu.VMEM((N_DP, SLOT, MODEL), BF16),
            pltpu.VMEM((N_DP, 8, 128), I32),
            pltpu.VMEM((N_DP, SLOT, MODEL), BF16),
            pltpu.VMEM((8, COLS), F32),
            pltpu.VMEM((8, COLS), F32),
            pltpu.VMEM((N_DP, CHIPS, 16, COLS), BF16),
            pltpu.VMEM((CHIP_TOK, MODEL), BF16),
            pltpu.VMEM((CHIP_TOK, HEAD_SIZE), F32),
            pltpu.VMEM((CHIP_TOK, HEAD_SIZE), F32),
            pltpu.VMEM((CHIP_TOK, QCOLS), BF16),
            pltpu.VMEM((PIECES // 2, CHIP_TOK, HEAD_SIZE), BF16),
            pltpu.VMEM((PASSING, PIECES // 2, CHIP_TOK, HEAD_SIZE), BF16),
            pltpu.VMEM((CHIP_TOK, 128), BF16),
            pltpu.VMEM((REACH + 1, CHIP_TOK, 128), BF16),
            pltpu.VMEM((8, 1, CHIP_TOK), F32),
            pltpu.VMEM((8, 1, CHIP_TOK), F32),
            pltpu.VMEM((8, HEAD_SIZE, CHIP_TOK), F32),
            pltpu.VMEM((CHIP_TOK, QCOLS), BF16),
            pltpu.SemaphoreType.DMA((N_COPIES,)),
            pltpu.SemaphoreType.DMA((N_COPIES,)),
            pltpu.SemaphoreType.DMA((PIECES, LEGS)),
            pltpu.SemaphoreType.DMA((PIECES, PASSING)),
            pltpu.SemaphoreType.DMA((4,)),
        ],
        compiler_params=pltpu.CompilerParams(
            collective_id=0, has_side_effects=True, vmem_limit_bytes=50 * 2**20
        ),
    )(tokens, qkv_weight, route.reshape(1, TOK), offset.reshape(1, TOK), doc_lengths, freq)


def solution(mesh):
    in_specs = (
        P(("dp", "sp"), None),
        P(("dp", "sp"), None),
        P(("dp", "sp")),
        P(("dp", "sp")),
        P("dp", None),
    )
    out_specs = P(("dp", "sp"), None)
    return jax.shard_map(
        on_device, mesh=mesh, in_specs=in_specs, out_specs=out_specs, check_vma=False
    )
```

```python
import jax
import jax.numpy as jnp
from jax import lax
from jax.experimental import pallas as pl
from jax.experimental.pallas import tpu as pltpu
from jax.sharding import PartitionSpec as P

HEAD_SIZE = 128
ROPE_BASE = 500000.0
N_DP = 8
SIDE = 4
CHIPS = SIDE * SIDE
TOK = 256
CHIP_TOK = 2 * TOK
MODEL = 2048
SLOT = TOK // N_DP
QCOLS = 1024
KVCOLS = 256
COLS = QCOLS + 2 * KVCOLS
HALF = COLS // 2
REACH = 4
HEADS_AT_ONCE = 4
DOCS = 16
PIECES = 8
CROSSING = (1, 3, 5)
LEGS = 12
PASSING = 5
BIG = 2.0**100
FACTOR = HEAD_SIZE ** (-0.5) * 1.4426950408889634
EXTRA_RIGHT, EXTRA_LEFT = 4, 3
W_RIGHT, W_LEFT = 3, 4
PIECE_ORDER = (0, 2, 4, 6, 1, 3, 7, 5)
ORDER = ((0, 1), (0, 0), (4, 0), (4, 1), (1, 0), (3, 0), (1, 1), (2, 0), (3, 1), (2, 1))
ARRIVALS = (
    (((0, 4), (2, 4),), ((0, 1), (0, 4), (2, 1), (2, 4),), ((0, 1), (0, 4), (2, 1), (2, 4),), ((0, 3), (0, 1), (0, 4), (2, 3), (2, 1), (2, 4),)),
    (((4, 4), (1, 5),), ((4, 1), (4, 4),), ((4, 1), (4, 4),), ((4, 3), (4, 1), (4, 4),)),
    (((0, 1), (6, 4), (3, 5), (1, 4), (2, 1), (5, 5), (3, 4), (0, 3),), ((0, 3), (6, 1), (6, 4), (2, 3), (1, 1), (1, 4), (4, 3), (3, 1), (3, 4),), ((0, 3), (6, 1), (6, 4), (1, 1), (1, 4), (2, 3), (3, 1), (3, 4),), ((6, 3), (6, 1), (6, 4), (1, 3), (1, 1), (1, 4), (3, 3), (3, 1), (3, 4),)),
    (((4, 1), (7, 4), (2, 3), (6, 1), (5, 4), (4, 3),), ((0, 2), (7, 1), (7, 4), (6, 3), (5, 1), (5, 4),), ((4, 3), (7, 1), (7, 4), (6, 3), (5, 1), (5, 4),), ((7, 3), (7, 1), (7, 4), (5, 3), (5, 1), (5, 4),)),
    (((1, 1), (1, 3), (0, 2), (3, 1),), ((1, 3),), ((1, 2), (0, 2),), ((0, 2), (1, 2), (1, 5),)),
    (((3, 3), (6, 3), (7, 1),), ((2, 2), (3, 3),), ((1, 3), (2, 2), (3, 2), (4, 2), (3, 3),), ((2, 2), (3, 2), (3, 5),)),
    (((5, 3), (2, 2), (5, 1), (4, 2), (1, 2),), ((1, 2), (4, 2),), ((6, 2), (7, 3),), ((4, 2), (5, 2), (5, 5), (6, 2),)),
    (((7, 3), (3, 2),), ((3, 2), (7, 3),), ((7, 2), (5, 2),), ((7, 2),)),
    (((6, 2), (5, 2),), ((6, 2), (5, 2), (5, 3),), ((5, 3),), ()),
    (((7, 2),), ((7, 2),), (), ()),
    ((), (), (), ()),
)
MESH = pl.DeviceIdType.MESH
F32 = jnp.float32
BF16 = jnp.bfloat16
I32 = jnp.int32


def iota(shape, dim):
    return lax.broadcasted_iota(I32, shape, dim)


class Copies:
    def __init__(self, send, recv):
        self.send, self.recv, self.made = send, recv, []

    def start(self, src, dst, device):
        n = len(self.made)
        copy = pltpu.make_async_remote_copy(
            src_ref=src,
            dst_ref=dst,
            send_sem=self.send.at[n],
            recv_sem=self.recv.at[n],
            device_id=device,
            device_id_type=MESH,
        )
        copy.start()
        self.made.append(copy)
        return copy

    def drain(self):
        for copy in self.made:
            copy.wait_send()


def greet(devices):
    barrier = pltpu.get_barrier_semaphore()
    for device in devices:
        pl.semaphore_signal(barrier, inc=1, device_id=device, device_id_type=MESH)
    return lambda: pl.semaphore_wait(barrier, len(devices))


N_COPIES = 1 + 7 + 7 + 2 * 7 + 2 * 2 * (4 + 16) + 4 + 2


def kernel(
    tokens, w, route, offset, lens, freq, out,
    packed, ids, got, got_ids, extra, wsend, wrecv, wbuf, x,
    cosine, sine, q, kv, kvbuf, qdoc, kdoc, top, total, acc, mine,
    send, recv, leg_send, leg_recv,
):
    z = lax.axis_index("dp")
    sp = lax.axis_index("sp")
    core = lax.rem(sp, 2)
    chip = sp // 2
    cy, cx = chip // SIDE, lax.rem(chip, SIDE)
    partner = (z, sp + 1 - 2 * core)

    def at_z(d):
        return (lax.rem(z + d + N_DP, N_DP), sp)

    def place(dy, dx):
        return lax.rem(cy + dy + SIDE, SIDE) * SIDE + lax.rem(cx + dx + SIDE, SIDE)

    def at_chip(dy, dx):
        return (z, place(dy, dx) * 2 + core)

    def half_of(c):
        cols = lambda base, width: w[:, pl.ds(pl.multiple_of(base + c * width, 128), width)]
        return [
            (0, QCOLS, cols(0, QCOLS)),
            (QCOLS, KVCOLS, cols(2 * QCOLS, KVCOLS)),
            (QCOLS + KVCOLS, KVCOLS, cols(2 * QCOLS + 2 * KVCOLS, KVCOLS)),
        ]

    met = greet(
        [at_z(d) for d in range(1, N_DP)]
        + [partner]
        + [at_chip(0, 1), at_chip(0, -1), at_chip(1, 0), at_chip(-1, 0)]
    )
    for base, width, part in half_of(1 - core):
        wsend[:, base : base + width] = part.astype(F32)

    met()
    copies = Copies(send, recv)

    swap = copies.start(wsend, wrecv, partner)

    group = iota((8, TOK), 0)
    route_row = route[...]
    onehot = route_row == group
    before = (iota((TOK, TOK), 0) < iota((TOK, TOK), 1)).astype(F32).astype(BF16)
    rank = jnp.dot(
        onehot.astype(F32).astype(BF16), before, preferred_element_type=F32
    ).astype(I32)
    dest = jnp.where(rank < SLOT, group * SLOT + rank, N_DP * SLOT + rank - SLOT)
    dest = jnp.sum(jnp.where(onehot, dest, 0), axis=0, keepdims=True)

    def pack(block):
        pick = (iota((SLOT, TOK), 0) + block * SLOT == dest).astype(F32).astype(BF16)
        return jnp.dot(pick, tokens[...], preferred_element_type=F32).astype(BF16)

    def extra_ring(s):
        sent = []
        right, left = lax.rem(z - s + N_DP, N_DP), lax.rem(z + s, N_DP)
        if s < EXTRA_RIGHT:
            sent.append(copies.start(extra.at[right], extra.at[right], at_z(1)))
        if s < EXTRA_LEFT:
            sent.append(copies.start(extra.at[left], extra.at[left], at_z(-1)))
        return sent

    def w_ring(s):
        sent = []
        if s < W_RIGHT:
            here, there = (1 - s) % N_DP, -s % N_DP
            sent.append(copies.start(wbuf.at[here, chip], wbuf.at[there, chip], at_z(1)))
        if s < W_LEFT:
            sent.append(copies.start(wbuf.at[1 + s, chip], wbuf.at[2 + s, chip], at_z(-1)))
        return sent

    facts = jnp.where(
        group == 0,
        offset[...] - sp * TOK,
        jnp.where(group == 1, route_row, jnp.where(group == 2, 1, 0)),
    ).astype(F32).astype(BF16)
    lane = iota((TOK, TOK), 0) - z * SLOT
    lane_ok = jnp.where((lane >= 0) & (lane < SLOT), lane, -10 * TOK)

    def numbers_of(block):
        pick = (lane_ok + block * SLOT == dest).astype(F32).astype(BF16)
        found = lax.dot_general(
            facts, pick, (((1,), (1,)), ((), ())), preferred_element_type=F32
        ).astype(I32)
        number = found[1:2] * TOK + found[0:1] + found[2:3]
        return [number[:, 0:128], number[:, 128:256]]

    more = numbers_of(N_DP) + [jnp.zeros((4, 128), I32)]

    def prepare(d):
        to = lax.rem(z + d, N_DP)
        packed[to] = pack(to)
        ids[to] = jnp.concatenate(numbers_of(to) + more, axis=0)

    tokens_sent = []

    def send_tokens(d):
        to = lax.rem(z + d, N_DP)
        tokens_sent.append(copies.start(packed.at[to], got.at[z], at_z(d)))
        tokens_sent.append(copies.start(ids.at[to], got_ids.at[z], at_z(d)))

    for d in (1, 7):
        prepare(d)
        send_tokens(d)

    swap.wait_recv()
    for base, width, part in half_of(core):
        own = part.astype(F32)
        other = wrecv[:, base : base + width]
        first = jnp.where(core == 0, own, other)
        second = jnp.where(core == 0, other, own)
        wbuf[1, chip, :, base : base + width] = jnp.concatenate([first, second], axis=0).astype(BF16)
    w_tour = w_ring(0)

    extra[z] = pack(N_DP)
    tour = extra_ring(0)

    def w_step(s):
        for copy in w_tour:
            copy.wait_recv()
        return w_ring(s)

    def extra_step(s):
        for copy in tour:
            copy.wait_recv()
        return extra_ring(s)

    class Plane:
        def __init__(self, which, first, second, low, middle, high):
            self.which, self.first, self.second = which, first, second
            self.all, self.one, self.two = (low, high), (low, middle), (middle, high)

        def at(self, a, b):
            return (a * self.first[0] + b * self.second[0], a * self.first[1] + b * self.second[1])

        def send(self, a, b, blocks, to):
            ref = wbuf.at[
                pl.ds(blocks[0], blocks[1] - blocks[0]), place(*self.at(a, b)), :, pl.ds(self.which * HALF, HALF)
            ]
            return copies.start(ref, ref, at_chip(*self.at(*to)))

        def open(self):
            self.near = [self.send(0, 0, self.all, (1, 0)), self.send(0, 0, self.all, (-1, 0))]
            self.across = {}

        def spread(self, u):
            self.across[u] = [self.send(u, 0, self.all, (0, 1)), self.send(u, 0, self.all, (0, -1))]

        def forward(self):
            self.near[0].wait_recv()
            self.far = [self.send(-1, 0, self.one, (1, 0))]
            self.near[1].wait_recv()
            self.far.append(self.send(1, 0, self.two, (-1, 0)))

        def close(self):
            for copy in self.far:
                copy.wait_recv()

        def pass_on(self, u):
            self.across[u][0].wait_recv()
            one = self.send(u, -1, self.one, (0, 1))
            self.across[u][1].wait_recv()
            return [one, self.send(u, 1, self.two, (0, -1))]

    near, rest = (
        [Plane(0, (0, 1), (1, 0), *blocks), Plane(1, (1, 0), (0, 1), *blocks)]
        for blocks in ((0, 2, 3), (3, 5, 8))
    )
    last = []

    def open_plane(planes):
        for plane in planes:
            plane.open()
        for plane in planes:
            plane.spread(0)

    def widen(planes):
        for plane in planes:
            plane.forward()
        for plane in planes:
            plane.spread(-1)
            plane.spread(1)

    def finish(planes):
        for plane in planes:
            plane.close()
            plane.spread(2)

    def pass_on(planes, u):
        for plane in planes:
            last.extend(plane.pass_on(u))

    w_tour = w_step(1)
    open_plane(near)
    for d in (3, 2):
        prepare(d)
    tour = extra_step(1)
    widen(near)
    w_tour = w_step(2)
    tour = extra_step(2)
    send_tokens(3)
    for d in (5, 6, 4):
        prepare(d)
    finish(near)
    pass_on(near, 0)
    w_tour = w_step(3)
    send_tokens(5)
    send_tokens(2)
    pass_on(near, -1)
    tour = extra_step(3)
    send_tokens(6)
    send_tokens(4)
    pass_on(near, 1)
    w_tour = w_step(4)
    open_plane(rest)
    pass_on(near, 2)
    prepare(0)
    got[z] = packed[z]
    got_ids[z] = ids[z]

    lanes = iota((1, 128), 1)
    starts = jnp.full((1, 128), 2**30, I32)
    ends = jnp.full((1, 128), 2**30, I32)
    row = iota((CHIP_TOK, 128), 0) + chip * CHIP_TOK
    begin_of = jnp.zeros((CHIP_TOK, 128), I32)
    begin = lens[0, 0] * 0
    for e in range(DOCS):
        starts = jnp.where(lanes == e, begin, starts)
        begin_of = jnp.where(row >= begin, begin, begin_of)
        begin = begin + lens[0, e]
        ends = jnp.where(lanes == e, begin, ends)
    angle = (row - begin_of).astype(F32) * freq[...]
    cosine[...] = jnp.cos(angle)
    sine[...] = jnp.sin(angle) * jnp.where(lanes < 64, -1.0, 1.0)

    def member(base):
        point = iota((CHIP_TOK, 128), 0) + base
        return (point >= starts) & (point < ends)

    qdoc[...] = jnp.where(member(chip * CHIP_TOK), 1.0, 0.0).astype(BF16)
    for d in range(REACH + 1):
        kdoc[d] = jnp.where(member((chip - d) * CHIP_TOK), 0.0, -BIG).astype(BF16)

    widen(rest)
    finish(rest)
    pass_on(rest, 0)
    tour = extra_step(4)
    for u in (-1, 1, 2):
        pass_on(rest, u)

    for copy in tokens_sent:
        copy.wait_recv()
    mine_ids = iota((TOK, TOK), 0) + z * TOK + 1
    numbers = jnp.zeros((8, 128), I32)
    for source in range(N_DP):
        numbers += got_ids[source]
    to_place = [
        (jnp.concatenate([numbers[n : n + 1], numbers[n + 1 : n + 2]], axis=1) == mine_ids)
        .astype(F32)
        .astype(BF16)
        for n in (0, 2)
    ]
    own_rows = pl.ds(pl.multiple_of(core * TOK, TOK), TOK)
    other_rows = pl.ds(pl.multiple_of((1 - core) * TOK, TOK), TOK)
    shared = []
    for part in range(N_DP):
        from_z = lax.rem(z + part + N_DP - 1, N_DP)
        cols = pl.ds(pl.multiple_of(from_z * 256, 256), 256)
        rows = jnp.dot(
            to_place[0], got[:, :, cols].reshape(TOK, 256), preferred_element_type=F32
        ) + jnp.dot(
            to_place[1], extra[:, :, cols].reshape(TOK, 256), preferred_element_type=F32
        )
        x[own_rows, part * 256 : part * 256 + 256] = rows.astype(BF16)
        if part % 2:
            ready = x.at[own_rows, part * 256 - 256 : part * 256 + 256]
            shared.append(copies.start(ready, ready, partner))
    for copy in last:
        copy.wait_recv()

    def project(c, rows):
        cols = pl.ds(pl.multiple_of(c * 256, 256), 256)
        weights = wbuf[:, :, :, cols].reshape(MODEL, 256)
        return jnp.dot(x[rows], weights, preferred_element_type=F32).astype(BF16)

    def rotated(y, rows):
        parts = []
        for n in range(2):
            v = y[:, n * 128 : n * 128 + 128].astype(F32)
            parts.append((v * cosine[rows] + pltpu.roll(v, 64, 1) * sine[rows]).astype(BF16))
        return parts

    def project_keys(rows, base):
        keys = rotated(project(4, rows), rows)
        values = project(5, rows).astype(F32)
        for g in range(2):
            kv[2 * g, rows] = keys[g]
            for t in range(2):
                block = values[t * 128 : t * 128 + 128, g * 128 : g * 128 + 128]
                at = pl.ds(pl.multiple_of(base + t * 128, 128), 128)
                kv[2 * g + 1, at] = block.T.astype(BF16)

    def queries(rows):
        def query(c, carry):
            for n, part in enumerate(rotated(project(c, rows), rows)):
                q[rows, pl.ds(pl.multiple_of(c * 256 + n * 128, 128), 128)] = part
            return carry

        lax.fori_loop(0, 4, query, 0)

    def piece(n):
        return n // 2, (own_rows, other_rows)[n % 2]

    def leg(n, number, d, to, source, when):
        copy = pltpu.make_async_remote_copy(
            src_ref=source,
            dst_ref=kvbuf.at[(d - 1, *piece(n))],
            send_sem=leg_send.at[n, number],
            recv_sem=leg_recv.at[n, d - 1],
            device_id=to,
            device_id_type=MESH,
        )
        return copy, when

    def legs(n):
        own, came = kv.at[piece(n)], lambda d: kvbuf.at[(d - 1, *piece(n))]
        right, left, down = at_chip(0, 1), at_chip(0, -1), at_chip(1, 0)
        inner = (cx == 1) | (cx == 2)
        first = [(4, down, own, None), (1, right, own, cx < 3), (3, left, own, cx == 0)]
        if n not in CROSSING:
            return {
                0: first,
                4: [(3, left, came(4), cx > 0), (1, right, came(4), cx == 3)],
                1: [(2, right, came(1), inner)],
                3: [(2, left, came(3), inner)],
            }
        return {
            0: first + [(PASSING, left, own, cx == 1)],
            4: [(3, left, came(4), cx > 1), (1, right, came(4), cx == 3)],
            1: [(2, right, came(1), cx == 0), (PASSING, down, came(1), cx == 3)],
            PASSING: [
                (2, left, came(PASSING), cx == 0),
                (3, down, came(PASSING), cx == 0),
                (2, right, came(PASSING), cx == 3),
            ],
            3: [(2, left, came(3), cx == 3)],
        }

    routes, number = [], 0
    for n in range(PIECES):
        number = 0
        route_of = {}
        for cause, parts in legs(n).items():
            route_of[cause] = []
            for d, to, source, when in parts:
                route_of[cause].append(leg(n, number, d, to, source, when))
                number += 1
        routes.append(route_of)

    def do(action, n, cause):
        for copy, when in routes[n].get(cause, []):
            run = copy.start if action == "start" else copy.wait_send
            if when is None:
                run()
            else:
                pl.when(when)(run)

    def arrived(n, d):
        wait = pltpu.make_async_remote_copy(
            src_ref=kvbuf.at[(d - 1, *piece(n))],
            dst_ref=kvbuf.at[(d - 1, *piece(n))],
            send_sem=leg_send.at[n, 0],
            recv_sem=leg_recv.at[n, d - 1],
            device_id=partner,
            device_id_type=MESH,
        ).wait_recv
        wait()
        do("start", n, d)

    project_keys(own_rows, core * TOK)
    for n in PIECE_ORDER[:4]:
        do("start", n, 0)
    queries(own_rows)
    for copy in shared:
        copy.wait_recv()
    project_keys(other_rows, (1 - core) * TOK)

    for n in PIECE_ORDER[4:]:
        do("start", n, 0)
    queries(other_rows)

    def block_step(d, g, heads, first, last):
        keys_of = kv.at[2 * g] if d == 0 else kvbuf.at[d - 1, 2 * g]
        values_of = kv.at[2 * g + 1] if d == 0 else kvbuf.at[d - 1, 2 * g + 1]
        chains = []
        for r in heads:
            h = g * 4 + r
            qcols = pl.ds(pl.multiple_of(h * 128, 128), 128)
            for half in range(2):
                lo, hi = 0, 512
                if d == 0 and half == 0:
                    hi = 256
                if d == REACH and half == 1:
                    lo = 256
                chains.append((h, qcols, slice(half * 256, half * 256 + 256), half, lo, hi))
        scores, old = [], []
        for h, qcols, qs, half, lo, hi in chains:
            keys = jnp.concatenate([keys_of[lo:hi], kdoc[d, lo:hi]], axis=1)
            query = jnp.concatenate([q[qs, qcols], qdoc[qs]], axis=1)
            s = lax.dot_general(
                keys, query, (((1,), (1,)), ((), ())), preferred_element_type=F32
            )
            if d == 0:
                n = hi - lo
                seen = iota((n, 256), 0) + lo <= iota((n, 256), 1) + half * 256
                s = jnp.where(seen, s, -BIG)
            scores.append(s)
            if not first:
                old.append((top[h, :, qs], total[h, :, qs], acc[h, :, qs]))
        new = []
        for n, (h, qcols, qs, half, lo, hi) in enumerate(chains):
            s = scores[n]
            best = jnp.max(s, axis=0, keepdims=True)
            if not first:
                best = jnp.maximum(old[n][0], best)
                alpha = jnp.exp2((old[n][0] - best) * FACTOR)
            e = jnp.exp2((s - best) * FACTOR)
            part = jnp.sum(e, axis=0, keepdims=True)
            values = jnp.concatenate(
                [values_of[t : t + 128] for t in range(lo, hi, 128)], axis=1
            )
            pv = jnp.dot(values, e.astype(BF16), preferred_element_type=F32)
            if not first:
                part = old[n][1] * alpha + part
                pv = old[n][2] * alpha + pv
            new.append((best, part, pv))
        for (best, part, pv), (h, qcols, qs, half, lo, hi) in zip(new, chains):
            if last:
                mine[qs, qcols] = (pv / part).T.astype(BF16)
            else:
                top[h, :, qs] = best
                total[h, :, qs] = part
                acc[h, :, qs] = pv

    def attend(d, g, first=False, last=False):
        def heads(r, carry):
            block_step(d, g, [r * HEADS_AT_ONCE + n for n in range(HEADS_AT_ONCE)], first, last)
            return carry

        lax.fori_loop(0, 4 // HEADS_AT_ONCE, heads, 0)

    out_cols = lambda g: pl.ds(pl.multiple_of(core * QCOLS + g * 512, 512), 512)

    def give(g):
        cols = slice(g * 512, g * 512 + 512)
        return copies.start(mine.at[other_rows, cols], out.at[:, out_cols(g)], partner)

    def arrive(step):
        for column, events in enumerate(ARRIVALS[step]):
            if events:

                @pl.when(cx == column)
                def _(events=events):
                    for n, d in events:
                        arrived(n, d)

    back = []
    for step, (d, g) in enumerate(ORDER):
        arrive(step)
        attend(d, g, first=d == 0, last=d == 2)
        if d == 2:
            back.append(give(g))
    for g in range(2):
        out[:, out_cols(g)] = mine[own_rows, g * 512 : g * 512 + 512]
    arrive(len(ORDER))
    for copy in back:
        copy.wait_recv()
    copies.drain()
    for n in range(PIECES):
        for cause in routes[n]:
            do("wait", n, cause)


def on_device(tokens, qkv_weight, route, offset, doc_lengths):
    half = HEAD_SIZE // 2
    freq = ROPE_BASE ** (-(jnp.arange(half, dtype=F32) * 2.0 / HEAD_SIZE))
    freq = jnp.concatenate([freq, freq])[None]
    vmem = pl.BlockSpec(memory_space=pltpu.VMEM)
    smem = pl.BlockSpec(memory_space=pltpu.SMEM)
    return pl.pallas_call(
        kernel,
        out_shape=jax.ShapeDtypeStruct((TOK, 2 * QCOLS), BF16),
        in_specs=[vmem, vmem, vmem, vmem, smem, vmem],
        out_specs=vmem,
        scratch_shapes=[
            pltpu.VMEM((N_DP, SLOT, MODEL), BF16),
            pltpu.VMEM((N_DP, 8, 128), I32),
            pltpu.VMEM((N_DP, SLOT, MODEL), BF16),
            pltpu.VMEM((N_DP, 8, 128), I32),
            pltpu.VMEM((N_DP, SLOT, MODEL), BF16),
            pltpu.VMEM((8, COLS), F32),
            pltpu.VMEM((8, COLS), F32),
            pltpu.VMEM((N_DP, CHIPS, 16, COLS), BF16),
            pltpu.VMEM((CHIP_TOK, MODEL), BF16),
            pltpu.VMEM((CHIP_TOK, HEAD_SIZE), F32),
            pltpu.VMEM((CHIP_TOK, HEAD_SIZE), F32),
            pltpu.VMEM((CHIP_TOK, QCOLS), BF16),
            pltpu.VMEM((PIECES // 2, CHIP_TOK, HEAD_SIZE), BF16),
            pltpu.VMEM((PASSING, PIECES // 2, CHIP_TOK, HEAD_SIZE), BF16),
            pltpu.VMEM((CHIP_TOK, 128), BF16),
            pltpu.VMEM((REACH + 1, CHIP_TOK, 128), BF16),
            pltpu.VMEM((8, 1, CHIP_TOK), F32),
            pltpu.VMEM((8, 1, CHIP_TOK), F32),
            pltpu.VMEM((8, HEAD_SIZE, CHIP_TOK), F32),
            pltpu.VMEM((CHIP_TOK, QCOLS), BF16),
            pltpu.SemaphoreType.DMA((N_COPIES,)),
            pltpu.SemaphoreType.DMA((N_COPIES,)),
            pltpu.SemaphoreType.DMA((PIECES, LEGS)),
            pltpu.SemaphoreType.DMA((PIECES, PASSING)),
        ],
        compiler_params=pltpu.CompilerParams(
            collective_id=0, has_side_effects=True, vmem_limit_bytes=50 * 2**20
        ),
    )(tokens, qkv_weight, route.reshape(1, TOK), offset.reshape(1, TOK), doc_lengths, freq)


def solution(mesh):
    in_specs = (
        P(("dp", "sp"), None),
        P(("dp", "sp"), None),
        P(("dp", "sp")),
        P(("dp", "sp")),
        P("dp", None),
    )
    out_specs = P(("dp", "sp"), None)
    return jax.shard_map(
        on_device, mesh=mesh, in_specs=in_specs, out_specs=out_specs, check_vma=False
    )
```
